128 devices in a mesh: seq: 32 (over z, y, core), tp: 4 (over x).
Axes of the slice: x: 4, y: 4, z: 4, core: 2. Of those that a mesh axis runs over, the one named last changes fastest.
Arguments:
- pool_keys: bfloat16 [4096, 16, 1024], P(('seq', 'tp')), may hold values from -6 to 6
- pool_values: bfloat16 [4096, 16, 1024], P(('seq', 'tp')), may hold values from -6 to 6
- passage_ids: int32 [16], replicated, may hold values from 0 to 31, as said below
- page_slot: int32 [32, 128], replicated, may hold values from 0 to 4095, as said below
- offsets: int32 [16], replicated, may hold values from 0 to 33168, as said below
- recompute_blocks: int32 [16, 2], replicated, may hold values from 0 to 15, as said below
- hidden_rows: bfloat16 [4096, 8192], P('seq'), may hold values from -6 to 6
- w_key: bfloat16 [8192, 1024], P(None, 'tp'), may hold values from -0.0625 to 0.0625
- w_value: bfloat16 [8192, 1024], P(None, 'tp'), may hold values from -0.0625 to 0.0625
- queries: bfloat16 [4096, 8192], P('seq', 'tp'), may hold values from -200 to 200
Outputs:
- key_cache: bfloat16 [32768, 1024], P('seq', 'tp')
- value_cache: bfloat16 [32768, 1024], P('seq', 'tp')
- attended: bfloat16 [4096, 8192], P('seq', 'tp')
The draws below stay inside these ranges and needn't reach their ends.
Inputs may be any that keep to these rules, and one draw needn't show every extreme that they name: `passage_ids`: 16 different pool passage numbers. `page_slot`: every pool slot holds exactly one page. Group the slots by seq index: the slots from s * 2 * 64 on, 128 of them, lie on the devices of seq index s. Among the pages of the passages named in passage_ids, those of one such group that fall on the 1024 tokens of one seq index number at most 4, and the tokens of every seq index receive exactly 4 pages from some group. offsets[0] is below 1024 and each next offset exceeds the one before by 2048 to 2143. `recompute_blocks`: each row holds 2 different block numbers, in rising order.
All inputs are finite; a program needn't handle non-finite values.
Results may differ from the reference program's by a relative error of at most 0.019.
Values may be sent and summed in bfloat16 or wider, within the bound.
A program may use at most 192 MiB of HBM per device.

```python
import math
import jax
import jax.numpy as jnp
from jax import lax

HQ = 64
KVH = 8
HD = 128
D = 8192
PASSAGE_LEN = 2048
BLOCK = 128
PAGE = 16
RB = 2
TOK_DEV = 1024
PASSAGES = 16
SEQ = 32768
POOL_PASSAGES = 32
PAGES_PASSAGE = 128
BLOCKS_PASSAGE = 16
RECOMPUTE_ROWS = 4096
CAP = 4
N_SEQ = 32


def layout(key):
    pick_key, ticket_key, force_key, order_key, label_key, slot_key = jax.random.split(key, 6)
    per_dest = TOK_DEV // PAGE
    tickets = N_SEQ * CAP
    row_pages = 2 * per_dest
    middle = (jax.random.permutation(pick_key, POOL_PASSAGES - 2) + 1).astype(jnp.int32)
    ends = jnp.array([0, POOL_PASSAGES - 1], dtype=jnp.int32)
    chosen_set = jnp.concatenate([ends, middle[:PASSAGES - 2]])
    chosen_ids = chosen_set[jax.random.permutation(jax.random.fold_in(pick_key, 7), PASSAGES)].astype(jnp.int32)
    spare_ids = middle[PASSAGES - 2:]
    scores = jax.vmap(lambda sub_key: jax.random.permutation(sub_key, tickets))(jax.random.split(ticket_key, N_SEQ)).astype(jnp.int32)
    forced = jax.random.randint(force_key, (N_SEQ, 1), 0, N_SEQ)
    ticket_ids = jnp.arange(tickets, dtype=jnp.int32)[None, :]
    scores = jnp.where(ticket_ids // CAP == forced, scores - tickets, scores)
    winners = jnp.argsort(scores, axis=1)[:, :per_dest].astype(jnp.int32)
    shuffle = jax.vmap(lambda sub_key: jax.random.permutation(sub_key, per_dest))(jax.random.split(order_key, N_SEQ))
    source_row = (jnp.take_along_axis(winners, shuffle, axis=1) // CAP).astype(jnp.int32)
    counts = jnp.sum(source_row.reshape(-1)[:, None] == jnp.arange(N_SEQ, dtype=jnp.int32)[None, :], axis=0)
    room_left = jnp.cumsum(row_pages - counts)
    spare_total = N_SEQ * per_dest
    labels = jnp.sum(room_left[None, :] <= jnp.arange(spare_total, dtype=jnp.int32)[:, None], axis=1).astype(jnp.int32)
    labels = labels[jax.random.permutation(label_key, spare_total)]
    page_rows = jnp.zeros((POOL_PASSAGES, PAGES_PASSAGE), jnp.int32)
    page_rows = page_rows.at[chosen_ids].set(source_row.reshape(PASSAGES, PAGES_PASSAGE))
    page_rows = page_rows.at[spare_ids].set(labels.reshape(POOL_PASSAGES - PASSAGES, PAGES_PASSAGE))
    page_total = POOL_PASSAGES * PAGES_PASSAGE
    sort_key = page_rows.reshape(-1) * page_total + jax.random.permutation(slot_key, page_total).astype(jnp.int32)
    placed = jnp.argsort(sort_key).astype(jnp.int32)
    slot_table = jnp.zeros((page_total,), jnp.int32).at[placed].set(jnp.arange(page_total, dtype=jnp.int32))
    return (chosen_ids, slot_table.reshape(POOL_PASSAGES, PAGES_PASSAGE))


def draw_passage_ids(key, part):
    shared = layout(key)
    return shared[0]


def draw_page_slot(key, part):
    shared = layout(key)
    return shared[1]


def draw_offsets(key, part):
    key = jax.random.fold_in(key, 3)
    lead_key, gap_key = jax.random.split(key)
    leading = jax.random.randint(lead_key, (1,), 0, 1024)
    gaps = jax.random.randint(gap_key, (PASSAGES,), 0, 96)
    gaps = gaps.at[0].set(0)
    return (leading + jnp.arange(PASSAGES, dtype=jnp.int32) * PASSAGE_LEN + jnp.cumsum(gaps)).astype(jnp.int32)


def draw_recompute_blocks(key, part):
    key = jax.random.fold_in(key, 4)
    picks = jax.vmap(lambda sub_key: jax.random.permutation(sub_key, BLOCKS_PASSAGE)[:RB])(jax.random.split(key, PASSAGES))
    return jnp.sort(picks, axis=1).astype(jnp.int32)


def draw_queries(key, part):
    key = jax.random.fold_in(key, 5)
    normal_key = jax.random.fold_in(key, 0)
    values = jnp.clip(jax.random.normal(normal_key, (RECOMPUTE_ROWS, HQ * HD), jnp.float32) * 2.5, -15.0, 15.0)
    return values.astype(jnp.bfloat16)


def levels(rng, shape, shards, low, high):
    def one(position, parts):
        heights = jax.random.uniform(jax.random.fold_in(jax.random.fold_in(rng, 6), position), (parts,), jnp.float32, low / len(shards), high / len(shards))
        return jnp.repeat(jnp.exp(heights), shape[position] // parts).reshape((-1,) + (1,) * (len(shape) - position - 1))

    factor_of = one(*shards[0])
    for cut in shards[1:]:
        factor_of = factor_of * one(*cut)
    return factor_of


def gaussian(own_key, dims, deviation, reach, cuts=(), kind=jnp.bfloat16):
    entries = deviation * jax.random.normal(own_key, dims, jnp.float32)
    if cuts:
        entries = entries * levels(own_key, dims, cuts, -0.22, 0.18)
    return jnp.clip(entries, -reach, reach).astype(kind)


def setup_inputs(seed: int = 0) -> dict:
    key_list = jax.random.split(jax.random.key(seed), 11)
    return {
        "pool_keys": gaussian(key_list[0], (POOL_PASSAGES * PAGES_PASSAGE, PAGE, KVH * HD), 1.0, 6.0, ((0, 128),)),
        "pool_values": gaussian(key_list[1], (POOL_PASSAGES * PAGES_PASSAGE, PAGE, KVH * HD), 1.0, 6.0, ((0, 128),)),
        "passage_ids": draw_passage_ids(jax.random.fold_in(key_list[10], 71), 0),
        "page_slot": draw_page_slot(jax.random.fold_in(key_list[10], 71), 0),
        "offsets": draw_offsets(jax.random.fold_in(key_list[10], 71), 0),
        "recompute_blocks": draw_recompute_blocks(jax.random.fold_in(key_list[10], 71), 0),
        "hidden_rows": gaussian(key_list[6], (RECOMPUTE_ROWS, D), 1.0, 6.0, ((0, 32),)),
        "w_key": gaussian(key_list[7], (D, KVH * HD), D ** -0.5, 0.0625, ((1, 4),)),
        "w_value": gaussian(key_list[8], (D, KVH * HD), D ** -0.5, 0.0625, ((1, 4),)),
        "queries": draw_queries(jax.random.fold_in(key_list[10], 71), 0),
    }


MASKED = -1e+30

def frequencies():
    exponent = jnp.arange(0, HD, 2, dtype=jnp.float32) / HD
    base_rate = jnp.power(jnp.float32(500000.0), -exponent)
    wave_length = 2.0 * math.pi / base_rate
    smooth = (8192.0 / wave_length - 1.0) / 3.0
    blended = (1.0 - smooth) * base_rate / 8.0 + smooth * base_rate
    return jnp.where(wave_length > 8192.0, base_rate / 8.0, jnp.where(wave_length < 2048.0, base_rate, blended))

def rotate(values, places):
    row_count = values.shape[0]
    rate_table = frequencies()
    angles = places.astype(jnp.float32)[:, None] * rate_table[None, :]
    cosine = jnp.cos(angles)[:, None, :]
    sine_part = jnp.sin(angles)[:, None, :]
    per_head = values.reshape(row_count, -1, HD)
    first_half = per_head[..., :HD // 2]
    second_half = per_head[..., HD // 2:]
    turned = jnp.concatenate([first_half * cosine - second_half * sine_part, second_half * cosine + first_half * sine_part], axis=-1)
    return turned.reshape(row_count, -1)

def attend_rows(row_block, turned, row_seq, key_cache, value_cache):
    group_size = HQ // KVH
    scale_factor = 1.0 / math.sqrt(HD)
    passage_index = (row_block % PASSAGES).astype(jnp.int32)
    query_block = lax.dynamic_slice_in_dim(turned, row_block * BLOCK, BLOCK, 0).astype(jnp.float32).reshape(BLOCK, KVH, group_size, HD)
    seen_rows = lax.dynamic_slice_in_dim(row_seq, row_block * BLOCK, BLOCK, 0)
    key_span = jnp.arange(PASSAGE_LEN, dtype=jnp.int32)

    def visit_keys(key_passage, carry_in):
        row_peak, weight_sum, weighted = carry_in
        first_key = (key_passage * PASSAGE_LEN).astype(jnp.int32)
        key_block = lax.dynamic_slice_in_dim(key_cache, first_key, PASSAGE_LEN, 0).astype(jnp.float32).reshape(PASSAGE_LEN, KVH, HD)
        value_block = lax.dynamic_slice_in_dim(value_cache, first_key, PASSAGE_LEN, 0).astype(jnp.float32).reshape(PASSAGE_LEN, KVH, HD)
        scores = jnp.einsum('qhgd,khd->hgqk', query_block, key_block) * scale_factor
        allowed = seen_rows[None, None, :, None] >= (first_key + key_span)[None, None, None, :]
        scores = jnp.where(allowed, scores, MASKED)
        new_peak = jnp.maximum(row_peak, lax.optimization_barrier(jnp.max(scores, axis=3)))
        weights = jnp.where(allowed, jnp.exp(scores - new_peak[..., None]), 0.0)
        rescale = jnp.exp(row_peak - new_peak)
        weight_sum = weight_sum * rescale + lax.optimization_barrier(jnp.sum(weights, axis=3))
        rounded = lax.optimization_barrier(weights.astype(jnp.bfloat16)).astype(jnp.float32)
        weighted = weighted * rescale[..., None] + jnp.einsum('hgqk,khd->hgqd', rounded, value_block)
        return (new_peak, weight_sum, weighted)
    start_state = (jnp.full((KVH, group_size, BLOCK), MASKED, jnp.float32), jnp.zeros((KVH, group_size, BLOCK), jnp.float32), jnp.zeros((KVH, group_size, BLOCK, HD), jnp.float32))
    row_peak, weight_sum, weighted = lax.fori_loop(0, passage_index + 1, visit_keys, start_state)
    result = weighted / weight_sum[..., None]
    return result.transpose(2, 0, 1, 3).reshape(BLOCK, HQ * HD).astype(jnp.bfloat16)

def reference(pool_keys, pool_values, passage_ids, page_slot, offsets, recompute_blocks, hidden_rows, w_key, w_value, queries):
    slot_list = page_slot[passage_ids].reshape(-1)
    cached_keys = pool_keys[slot_list].reshape(SEQ, KVH * HD)
    cached_values = pool_values[slot_list].reshape(SEQ, KVH * HD)
    token_seq = jnp.arange(SEQ, dtype=jnp.int32)
    token_pos = offsets[token_seq // PASSAGE_LEN] + token_seq % PASSAGE_LEN
    rotated = rotate(cached_keys.astype(jnp.float32), token_pos).astype(jnp.bfloat16)
    row_ids = jnp.arange(RECOMPUTE_ROWS, dtype=jnp.int32)
    passage = row_ids // BLOCK % PASSAGES
    which_block = row_ids // (PASSAGES * BLOCK)
    in_block = row_ids % BLOCK
    block_start = recompute_blocks[passage, which_block] * BLOCK + in_block
    row_seq = (passage * PASSAGE_LEN + block_start).astype(jnp.int32)
    row_pos = (offsets[passage] + block_start).astype(jnp.int32)
    fresh_keys = rotate(jnp.dot(hidden_rows, w_key, preferred_element_type=jnp.float32), row_pos).astype(jnp.bfloat16)
    fresh_values = jnp.dot(hidden_rows, w_value, preferred_element_type=jnp.float32).astype(jnp.bfloat16)
    key_cache = rotated.at[row_seq].set(fresh_keys)
    value_cache = cached_values.at[row_seq].set(fresh_values)
    turned = rotate(queries.astype(jnp.float32), row_pos).astype(jnp.bfloat16)
    attended = lax.map(lambda row_block: attend_rows(row_block, turned, row_seq, key_cache, value_cache), jnp.arange(RECOMPUTE_ROWS // BLOCK, dtype=jnp.int32))
    return (key_cache, value_cache, attended.reshape(RECOMPUTE_ROWS, HQ * HD))
```

```python
import math

import jax
import jax.numpy as jnp
from jax import lax
from jax.experimental import pallas as pl
from jax.experimental.pallas import tpu as pltpu
from jax.sharding import PartitionSpec as P

HD = 128
PASSAGE_LEN = 2048
BLOCK = 128
PAGE = 16
RB = 2
TOK_DEV = 1024
CAP = 4
N_SEQ = 32
N_TP = 4
PASSAGES = 16
PER_DEST = TOK_DEV // PAGE
WIDTH = 256
HEADS = 16
MASKED = -1e30
EXPONENT = math.log2(math.e) / math.sqrt(HD)
QT = 256
UNIT = QT // BLOCK
BY_KEY = (((1,), (1,)), ((), ()))
MESH = pl.DeviceIdType.MESH


def frequencies():
    exponent = jnp.arange(0, HD, 2, dtype=jnp.float32) / HD
    base_rate = jnp.power(jnp.float32(500000.0), -exponent)
    wave_length = 2.0 * math.pi / base_rate
    smooth = (8192.0 / wave_length - 1.0) / 3.0
    blended = (1.0 - smooth) * base_rate / 8.0 + smooth * base_rate
    return jnp.where(
        wave_length > 8192.0, base_rate / 8.0, jnp.where(wave_length < 2048.0, base_rate, blended)
    )


def tables_at(places):
    rates = frequencies()
    angles = places.astype(jnp.float32)[:, None] * jnp.concatenate([rates, rates])[None, :]
    sign = jnp.where(jnp.arange(HD) < HD // 2, -1.0, 1.0).astype(jnp.float32)
    return jnp.cos(angles), jnp.sin(angles) * sign[None, :]


def lookup(small_table, wanted):
    matches = wanted[:, None] == jnp.arange(small_table.shape[0], dtype=jnp.int32)[None, :]
    return jnp.sum(jnp.where(matches, small_table[None, :], 0), axis=1)


def row_places(row_ids, recompute_blocks, offsets):
    passage = row_ids // BLOCK % PASSAGES
    which_block = row_ids // (PASSAGES * BLOCK)
    block_start = (
        lookup(recompute_blocks.reshape(-1), passage * RB + which_block) * BLOCK + row_ids % BLOCK
    )
    return lookup(offsets, passage) + block_start


def token_positions(first_token, offsets):
    token_seq = first_token + jnp.arange(TOK_DEV, dtype=jnp.int32)
    return lookup(offsets, token_seq // PASSAGE_LEN) + token_seq % PASSAGE_LEN


def turn(values, cosine, sine):
    return values * cosine + pltpu.roll(values, HD // 2, 1) * sine


def on_seq(source, target, send_sem, recv_sem, peer):
    return pltpu.make_async_remote_copy(
        src_ref=source,
        dst_ref=target,
        send_sem=send_sem,
        recv_sem=recv_sem,
        device_id={"seq": peer},
        device_id_type=MESH,
    )


def place(me):
    z = me // 8
    return z, (me // 2) % 4, me % 2, z % 2


def exchange_kernel(
    send_index, arrival, blend,
    pool_k, pool_v, fresh, queries, q_cos, q_sin, t_cos, t_sin,
    out_k, out_v, out_q,
    rows_k, rows_v, outgoing, arriving_k, arriving_v, turned, fresh_in,
    own_sem, tp_send, tp_recv, page_send, page_recv, q_send, q_recv, f_send, f_recv,
):
    me = lax.axis_index("seq")
    my_tp = lax.axis_index("tp")
    z, y, core, half = place(me)
    barrier = pltpu.get_barrier_semaphore()

    def greet_seq(step, _):
        pl.semaphore_signal(
            barrier, inc=1, device_id={"seq": lax.rem(me + step, N_SEQ)}, device_id_type=MESH
        )
        return 0

    lax.fori_loop(1, N_SEQ, greet_seq, 0)
    for step in range(1, N_TP):
        pl.semaphore_signal(
            barrier, inc=1, device_id={"tp": lax.rem(my_tp + step, N_TP)}, device_id_type=MESH
        )
    pl.semaphore_wait(barrier, N_SEQ - 1 + N_TP - 1)

    pools = (pool_k, pool_v)
    rows = (rows_k, rows_v)
    arriving = (arriving_k, arriving_v)

    def columns(which, owner):
        return pools[which].at[:, :, pl.ds(pl.multiple_of(owner * WIDTH, WIDTH), WIDTH)]

    def tp_copy(which, step):
        peer = lax.rem(my_tp + step, N_TP)
        return pltpu.make_async_remote_copy(
            src_ref=columns(which, peer),
            dst_ref=rows[which].at[pl.ds(my_tp * 32, 32)],
            send_sem=tp_send.at[which, step],
            recv_sem=tp_recv.at[which, step],
            device_id={"tp": peer},
            device_id_type=MESH,
        )

    def own_copy(which):
        return pltpu.make_async_copy(
            columns(which, my_tp), rows[which].at[pl.ds(my_tp * 32, 32)], own_sem.at[which]
        )

    for which in range(2):
        for step in (1, 3, 2):
            tp_copy(which, step).start()
        own_copy(which).start()

    for head in range(HEADS):
        cols = slice(head * HD, (head + 1) * HD)
        turned[head] = turn(
            queries[:, cols].astype(jnp.float32), q_cos[...], q_sin[...]
        ).astype(jnp.bfloat16)
    group_z = z - half + lax.rem(half + y // 2, 2)

    def q_dest(other_y):
        return group_z * 8 + other_y * 2 + core

    def q_remote(other_y):
        return on_seq(
            turned, out_q.at[y], q_send.at[other_y], q_recv.at[y], q_dest(other_y)
        )

    def q_local():
        return pltpu.make_async_copy(turned, out_q.at[y], q_recv.at[y])

    which_block = me // PASSAGES
    home = lax.rem(me, PASSAGES) * 2

    def f_remote(side):
        return on_seq(
            fresh, fresh_in.at[which_block], f_send.at[side], f_recv.at[which_block], home + side
        )

    def f_local():
        return pltpu.make_async_copy(fresh, fresh_in.at[which_block], f_recv.at[which_block])

    for side in range(2):

        @pl.when(home + side != me)
        def _():
            f_remote(side).start()

        @pl.when(home + side == me)
        def _():
            f_local().start()

    for other_y in range(4):

        @pl.when(q_dest(other_y) != me)
        def _():
            q_remote(other_y).start()

        @pl.when(q_dest(other_y) == me)
        def _():
            q_local().start()

    def page_copy(which, step):
        peer = lax.rem(me + step, N_SEQ)
        return on_seq(
            outgoing.at[which, peer],
            arriving[which].at[me],
            page_send.at[which, step],
            page_recv.at[which, step],
            peer,
        )

    for which in range(2):
        for step in range(1, N_TP):
            peer = lax.rem(my_tp + N_TP - step, N_TP)
            pltpu.make_async_remote_copy(
                src_ref=columns(which, my_tp),
                dst_ref=rows[which].at[pl.ds(peer * 32, 32)],
                send_sem=tp_send.at[which, step],
                recv_sem=tp_recv.at[which, step],
                device_id={"tp": peer},
                device_id_type=MESH,
            ).wait_recv()
        own_copy(which).wait()

        def pick(step, _):
            peer = lax.rem(me + step, N_SEQ)
            for rank in range(CAP):
                outgoing[which, peer, rank] = rows[which][send_index[peer * CAP + rank]]

            @pl.when(step > 0)
            def _():
                page_copy(which, step).start()

            return 0

        lax.fori_loop(0, N_SEQ, pick, 0)
        arriving[which][me] = outgoing[which, me]

    for slot in range(4):
        on_seq(turned, out_q.at[slot], q_send.at[0], q_recv.at[slot], me).wait_recv()
    for slot in range(2):
        on_seq(fresh, fresh_in.at[slot], f_send.at[0], f_recv.at[slot], me).wait_recv()

    for which in range(2):

        def landed(step, _):
            sender = lax.rem(me + N_SEQ - step, N_SEQ)
            on_seq(
                outgoing.at[which, me],
                arriving[which].at[sender],
                page_send.at[which, step],
                page_recv.at[which, step],
                sender,
            ).wait_recv()
            return 0

        lax.fori_loop(1, N_SEQ, landed, 0)

        def put(page, _):
            slot = arrival[page]
            block = page // 8
            where = pl.ds(pl.multiple_of(page * PAGE, PAGE), PAGE)
            within = pl.ds(pl.multiple_of(lax.rem(page, 8) * PAGE, PAGE), PAGE)
            got = arriving[which][slot // CAP, lax.rem(slot, CAP)]
            if which == 0:
                wide = got.astype(jnp.float32)
                cosine, sine = t_cos[where], t_sin[where]
                got = jnp.concatenate(
                    [
                        turn(wide[:, :HD], cosine, sine).astype(jnp.bfloat16),
                        turn(wide[:, HD:], cosine, sine).astype(jnp.bfloat16),
                    ],
                    axis=1,
                )
            new = fresh_in[blend[1, block], which, within]
            flag = jnp.full(got.shape, blend[0, block], jnp.int32) > 0
            mixed = jnp.where(flag, new.astype(jnp.float32), got.astype(jnp.float32))
            (out_k, out_v)[which][where] = mixed.astype(jnp.bfloat16)
            return 0

        lax.fori_loop(0, PER_DEST, put, 0)

    for which in range(2):
        for step in range(1, N_TP):
            tp_copy(which, step).wait_send()

        def sent(step, _):
            page_copy(which, step).wait_send()
            return 0

        lax.fori_loop(1, N_SEQ, sent, 0)
    for other_y in range(4):

        @pl.when(q_dest(other_y) != me)
        def _():
            q_remote(other_y).wait_send()

    for side in range(2):

        @pl.when(home + side != me)
        def _():
            f_remote(side).wait_send()


def attend_kernel(
    starts,
    own_k, own_v, q_ref,
    out_ref,
    k_buf, v_buf, acc, peak, part, stat, part_in, stat_in,
    own_sem, kv_send, kv_recv, side_send, side_recv, part_send, part_recv,
):
    me = lax.axis_index("seq")
    z, y, core, half = place(me)
    pair = z - half
    sibling = me + 1 - 2 * core
    barrier = pltpu.get_barrier_semaphore()

    def greet(step, _):
        pl.semaphore_signal(
            barrier, inc=1, device_id={"seq": lax.rem(me + step, N_SEQ)}, device_id_type=MESH
        )
        return 0

    lax.fori_loop(1, N_SEQ, greet, 0)
    pl.semaphore_wait(barrier, N_SEQ - 1)

    owns = (own_k, own_v)
    bufs = (k_buf, v_buf)

    def near(step):
        return lax.rem(z + step, 4)

    def at(level):
        return level * 8 + y * 2 + core

    def own_copy(which):
        return pltpu.make_async_copy(owns[which], bufs[which].at[z, core], own_sem.at[which])

    def kv_copy(which, step):
        return on_seq(
            owns[which], bufs[which].at[z, core], kv_send.at[which, step],
            kv_recv.at[which, step], at(near(step)),
        )

    def kv_landed(which, step):
        level = near(4 - step)
        return on_seq(
            owns[which], bufs[which].at[level, core], kv_send.at[which, step],
            kv_recv.at[which, step], at(level),
        )

    def side_copy(which, step):
        level = near(4 - step) if step else z
        source = bufs[which].at[level, core] if step else owns[which]
        return on_seq(
            source, bufs[which].at[level, core], side_send.at[which, step],
            side_recv.at[which, step], sibling,
        )

    def side_landed(which, step):
        level = near(4 - step) if step else z
        return on_seq(
            owns[which], bufs[which].at[level, 1 - core], side_send.at[which, step],
            side_recv.at[which, step], sibling,
        )

    for which in range(2):
        side_copy(which, 0).start()
        own_copy(which).start()
    for step in (1, 3, 2):
        for which in range(2):
            kv_copy(which, step).start()
    acc[...] = jnp.zeros_like(acc)
    peak[...] = jnp.full_like(peak, MASKED)

    ones = jnp.ones((PASSAGE_LEN, HD), jnp.bfloat16)

    def fold(slot, level, limit):
        def unit(index, _):
            for group in range(2):
                cols = slice(group * HD, (group + 1) * HD)
                heads = pl.ds(group * 8 + index * UNIT, UNIT)
                q = q_ref[slot, heads].reshape(QT, HD)
                keys = k_buf[level].reshape(PASSAGE_LEN, WIDTH)[:, cols]
                values = v_buf[level].reshape(PASSAGE_LEN, WIDTH)[:, cols]
                score = lax.dot_general(q, keys, BY_KEY, preferred_element_type=jnp.float32)
                if limit is not None:
                    token = lax.broadcasted_iota(jnp.int32, score.shape, 1)
                    row = lax.broadcasted_iota(jnp.int32, score.shape, 0) % BLOCK + limit
                    allowed = token <= row
                    score = jnp.where(allowed, score, MASKED)
                old = peak[slot, heads].reshape(QT, HD)
                new = jnp.maximum(old, jnp.max(score, axis=1, keepdims=True))
                keep = jnp.exp2((old - new) * EXPONENT)
                weight = jnp.exp2((score - new[:, :1]) * EXPONENT).astype(jnp.bfloat16)
                total = jnp.dot(
                    weight,
                    jnp.concatenate([values, ones], axis=1),
                    preferred_element_type=jnp.float32,
                )
                before = acc[slot, heads].reshape(QT, 2 * HD)
                acc[slot, heads] = (before * keep[:, :1] + total).reshape(UNIT, BLOCK, 2 * HD)
                peak[slot, heads] = new.reshape(UNIT, BLOCK, HD)
            return 0

        lax.fori_loop(0, 8 // UNIT, unit, 0)

    def slot_passage(slot):
        return lax.rem(half + slot // 2, 2) * 8 + 2 * slot + core

    def visit(slot, level):
        passage = level * 4 + y
        mine = slot_passage(slot)

        @pl.when(passage < mine)
        def _():
            fold(slot, level, None)

        @pl.when(passage == mine)
        def _():
            fold(slot, level, starts[slot])

    def owner(slot):
        return (pair + lax.rem(half + slot // 2, 2)) * 8 + slot * 2 + core

    def part_copies(slot):
        return (
            on_seq(part.at[slot], part_in.at[y], part_send.at[0, slot], part_recv.at[0, y],
                   owner(slot)),
            on_seq(stat.at[slot], stat_in.at[y], part_send.at[1, slot], part_recv.at[1, y],
                   owner(slot)),
        )

    def local_copies(slot):
        return (
            pltpu.make_async_copy(part.at[slot], part_in.at[y], part_recv.at[0, y]),
            pltpu.make_async_copy(stat.at[slot], stat_in.at[y], part_recv.at[1, y]),
        )

    def give_back(slot):
        lane = lax.broadcasted_iota(jnp.int32, (BLOCK, HD), 1)

        def head_part(head, logs):
            total = acc[slot, head]
            weight_sum = total[:, HD:]
            some = weight_sum > 0.0
            safe = jnp.where(some, weight_sum, 1.0)
            part[slot, head] = (total[:, :HD] / safe).astype(jnp.bfloat16)
            size = jnp.where(some, peak[slot, head] * EXPONENT + jnp.log2(safe), MASKED)
            return jnp.where(lane == head, size, logs)

        stat[slot] = lax.fori_loop(
            0, HEADS, head_part, jnp.full((BLOCK, HD), MASKED, jnp.float32)
        )

        @pl.when(owner(slot) != me)
        def _():
            for copy in part_copies(slot):
                copy.start()

        @pl.when(owner(slot) == me)
        def _():
            for copy in local_copies(slot):
                copy.start()

    for step in (0, 1, 3, 2):
        level = near(4 - step) if step else z
        for which in range(2):
            if step:
                kv_landed(which, step).wait_recv()
                side_copy(which, step).start()
            else:
                own_copy(which).wait()
        for which in range(2):
            side_landed(which, step).wait_recv()

        def each(slot, _):
            visit(slot, level)
            if step == 2:
                give_back(slot)
            return 0

        lax.fori_loop(0, 4, each, 0)

    for slot in range(4):
        on_seq(part.at[0], part_in.at[slot], part_send.at[0, 0], part_recv.at[0, slot],
               me).wait_recv()
        on_seq(stat.at[0], stat_in.at[slot], part_send.at[1, 0], part_recv.at[1, slot],
               me).wait_recv()
    logs = [stat_in[slot] for slot in range(4)]
    top = jnp.maximum(jnp.maximum(logs[0], logs[1]), jnp.maximum(logs[2], logs[3]))
    shares = [jnp.exp2(log - top) for log in logs]
    whole = 1.0 / (shares[0] + shares[1] + shares[2] + shares[3])
    shares = [share * whole for share in shares]
    for head in range(HEADS):
        result = sum(
            part_in[slot, head].astype(jnp.float32) * shares[slot][:, head : head + 1]
            for slot in range(4)
        )
        out_ref[:, head * HD : (head + 1) * HD] = result.astype(jnp.bfloat16)

    for which in range(2):
        for step in (1, 3, 2):
            kv_copy(which, step).wait_send()
        for step in range(4):
            side_copy(which, step).wait_send()
    for slot in range(4):

        @pl.when(owner(slot) != me)
        def _():
            for copy in part_copies(slot):
                copy.wait_send()


def on_device(
    pool_keys,
    pool_values,
    passage_ids,
    page_slot,
    offsets,
    recompute_blocks,
    hidden_rows,
    w_key,
    w_value,
    queries,
):
    me = lax.axis_index("seq")
    row_pages = N_TP * pool_keys.shape[0]
    used_slots = jnp.take(page_slot, passage_ids, axis=0).reshape(N_SEQ, PER_DEST)
    source_row = used_slots // row_pages
    row_local = used_slots % row_pages
    position_ids = jnp.arange(PER_DEST, dtype=jnp.int32)
    earlier = position_ids[None, :] < position_ids[:, None]
    same_source = source_row[:, :, None] == source_row[:, None, :]
    page_rank = jnp.sum(same_source & earlier[None, :, :], axis=2)
    slot_hit = (source_row == me)[:, :, None] & (
        page_rank[:, :, None] == jnp.arange(CAP, dtype=jnp.int32)[None, None, :]
    )
    send_index = jnp.sum(jnp.where(slot_hit, row_local[:, :, None], 0), axis=1).reshape(-1)
    my_source = lax.dynamic_index_in_dim(source_row, me, 0, keepdims=False)
    my_rank = lax.dynamic_index_in_dim(page_rank, me, 0, keepdims=False)
    arrival = my_source * CAP + my_rank

    passage = me // 2
    blocks = lax.dynamic_index_in_dim(recompute_blocks, passage, 0, keepdims=False)
    here = (me % 2) * 8 + jnp.arange(8, dtype=jnp.int32)
    hit = blocks[:, None] == here[None, :]
    blend = jnp.stack([jnp.any(hit, axis=0).astype(jnp.int32), hit[1].astype(jnp.int32)])

    row_pos = row_places(me * BLOCK + jnp.arange(BLOCK, dtype=jnp.int32), recompute_blocks, offsets)
    token_pos = token_positions(me * TOK_DEV, offsets)
    cosine, sine = tables_at(jnp.concatenate([row_pos, token_pos]))
    q_cos, t_cos = cosine[:BLOCK], cosine[BLOCK:]
    q_sin, t_sin = sine[:BLOCK], sine[BLOCK:]
    raw = jnp.dot(hidden_rows, w_key, preferred_element_type=jnp.float32).reshape(BLOCK, 2, HD)
    swapped = jnp.concatenate([raw[..., HD // 2 :], raw[..., : HD // 2]], axis=-1)
    fresh_keys = (raw * q_cos[:, None, :] + swapped * q_sin[:, None, :]).astype(jnp.bfloat16)
    fresh_values = jnp.dot(hidden_rows, w_value, preferred_element_type=jnp.float32).astype(
        jnp.bfloat16
    )
    fresh = jnp.stack([fresh_keys.reshape(BLOCK, WIDTH), fresh_values])

    vmem = pl.BlockSpec(memory_space=pltpu.VMEM)
    smem = pl.BlockSpec(memory_space=pltpu.SMEM)
    hbm = pl.BlockSpec(memory_space=pl.ANY)
    bf16 = jnp.bfloat16
    dma = pltpu.SemaphoreType.DMA
    key_cache, value_cache, q_group = pl.pallas_call(
        exchange_kernel,
        out_shape=[
            jax.ShapeDtypeStruct((TOK_DEV, WIDTH), bf16),
            jax.ShapeDtypeStruct((TOK_DEV, WIDTH), bf16),
            jax.ShapeDtypeStruct((4, HEADS, BLOCK, HD), bf16),
        ],
        in_specs=[smem, smem, smem, hbm, hbm, vmem, vmem, vmem, vmem, vmem, vmem],
        out_specs=[vmem, vmem, hbm],
        scratch_shapes=[
            pltpu.VMEM((128, PAGE, WIDTH), bf16),
            pltpu.VMEM((128, PAGE, WIDTH), bf16),
            pltpu.VMEM((2, N_SEQ, CAP, PAGE, WIDTH), bf16),
            pltpu.VMEM((N_SEQ, CAP, PAGE, WIDTH), bf16),
            pltpu.VMEM((N_SEQ, CAP, PAGE, WIDTH), bf16),
            pltpu.VMEM((HEADS, BLOCK, HD), bf16),
            pltpu.VMEM((RB, 2, BLOCK, WIDTH), bf16),
            dma((2,)),
            dma((2, N_TP)),
            dma((2, N_TP)),
            dma((2, N_SEQ)),
            dma((2, N_SEQ)),
            dma((4,)),
            dma((4,)),
            dma((2,)),
            dma((2,)),
        ],
        compiler_params=pltpu.CompilerParams(
            collective_id=0, has_side_effects=True, vmem_limit_bytes=48 * 2**20
        ),
        name="exchange",
    )(
        send_index, arrival, blend,
        pool_keys, pool_values, fresh, queries, q_cos, q_sin, t_cos, t_sin,
    )

    z, y, core, half = place(me)
    slots = jnp.arange(4, dtype=jnp.int32)
    slot_passages = ((half + slots // 2) % 2) * 8 + 2 * slots + core
    starts = lookup(recompute_blocks.reshape(-1), slot_passages * RB + z // 2) * BLOCK

    attended = pl.pallas_call(
        attend_kernel,
        out_shape=jax.ShapeDtypeStruct((BLOCK, HEADS * HD), bf16),
        in_specs=[smem, hbm, hbm, vmem],
        out_specs=vmem,
        scratch_shapes=[
            pltpu.VMEM((4, 2, TOK_DEV, WIDTH), bf16),
            pltpu.VMEM((4, 2, TOK_DEV, WIDTH), bf16),
            pltpu.VMEM((4, HEADS, BLOCK, 2 * HD), jnp.float32),
            pltpu.VMEM((4, HEADS, BLOCK, HD), jnp.float32),
            pltpu.VMEM((4, HEADS, BLOCK, HD), bf16),
            pltpu.VMEM((4, BLOCK, HD), jnp.float32),
            pltpu.VMEM((4, HEADS, BLOCK, HD), bf16),
            pltpu.VMEM((4, BLOCK, HD), jnp.float32),
            dma((2,)),
            dma((2, 4)),
            dma((2, 4)),
            dma((2, 4)),
            dma((2, 4)),
            dma((2, 4)),
            dma((2, 4)),
        ],
        compiler_params=pltpu.CompilerParams(
            collective_id=1, has_side_effects=True, vmem_limit_bytes=56 * 2**20
        ),
        name="attend",
    )(starts, key_cache, value_cache, q_group)
    return (key_cache, value_cache, attended)


def solution(mesh):
    placed = (
        P(("seq", "tp"), None, None),
        P(("seq", "tp"), None, None),
        P(),
        P(),
        P(),
        P(),
        P("seq", None),
        P(None, "tp"),
        P(None, "tp"),
        P("seq", "tp"),
    )
    return jax.shard_map(
        on_device,
        mesh=mesh,
        in_specs=placed,
        out_specs=(P("seq", "tp"), P("seq", "tp"), P("seq", "tp")),
        check_vma=False,
    )
```

```python
import math

import jax
import jax.numpy as jnp
from jax import lax
from jax.experimental import pallas as pl
from jax.experimental.pallas import tpu as pltpu
from jax.sharding import PartitionSpec as P

HD = 128
PASSAGE_LEN = 2048
BLOCK = 128
PAGE = 16
RB = 2
TOK_DEV = 1024
CAP = 4
N_SEQ = 32
N_TP = 4
PASSAGES = 16
PER_DEST = TOK_DEV // PAGE
WIDTH = 256
HEADS = 16
MASKED = -1e30
EXPONENT = math.log2(math.e) / math.sqrt(HD)
QT = 256
UNIT = QT // BLOCK
BY_KEY = (((1,), (1,)), ((), ()))
MESH = pl.DeviceIdType.MESH


def frequencies():
    exponent = jnp.arange(0, HD, 2, dtype=jnp.float32) / HD
    base_rate = jnp.power(jnp.float32(500000.0), -exponent)
    wave_length = 2.0 * math.pi / base_rate
    smooth = (8192.0 / wave_length - 1.0) / 3.0
    blended = (1.0 - smooth) * base_rate / 8.0 + smooth * base_rate
    return jnp.where(
        wave_length > 8192.0, base_rate / 8.0, jnp.where(wave_length < 2048.0, base_rate, blended)
    )


def turn(values, cosine, sine):
    return values * cosine + pltpu.roll(values, HD // 2, 1) * sine


def on_seq(source, target, send_sem, recv_sem, peer):
    return pltpu.make_async_remote_copy(
        src_ref=source,
        dst_ref=target,
        send_sem=send_sem,
        recv_sem=recv_sem,
        device_id={"seq": peer},
        device_id_type=MESH,
    )


def place(me):
    z = me // 8
    return z, (me // 2) % 4, me % 2, z % 2


def group_of(half, core):
    return lax.rem(half + core, 2)


def slot_half(group, slot):
    return lax.rem(group + slot, 2)


def rotation(first, count, rates):
    places = lax.broadcasted_iota(jnp.int32, (count, HD), 0) + first
    angles = places.astype(jnp.float32) * rates
    sine = jnp.sin(angles)
    lane = lax.broadcasted_iota(jnp.int32, (count, HD), 1)
    return jnp.cos(angles), jnp.where(lane < HD // 2, -sine, sine)


def exchange_kernel(
    passage_ids, page_slot, offsets, recompute_blocks, rates,
    pool_k, pool_v, hidden, w_key, w_value, queries,
    out_k, out_v, out_q,
    rows_k, rows_v, outgoing, arriving_k, arriving_v, turned, fresh, fresh_in,
    hidden_buf, w_buf, t_cos, t_sin, used, send_tab, arrival_tab, send_index, arrival,
    own_sem, load_sem, tp_send, tp_recv, page_send, page_recv, q_send, q_recv, f_send, f_recv,
):
    me = lax.axis_index("seq")
    my_tp = lax.axis_index("tp")
    z, y, core, half = place(me)
    barrier = pltpu.get_barrier_semaphore()

    def greet_seq(step, _):
        pl.semaphore_signal(
            barrier, inc=1, device_id={"seq": lax.rem(me + step, N_SEQ)}, device_id_type=MESH
        )
        return 0

    lax.fori_loop(1, N_SEQ, greet_seq, 0)
    for step in range(1, N_TP):
        pl.semaphore_signal(
            barrier, inc=1, device_id={"tp": lax.rem(my_tp + step, N_TP)}, device_id_type=MESH
        )
    pl.semaphore_wait(barrier, N_SEQ - 1 + N_TP - 1)

    pools = (pool_k, pool_v)
    rows = (rows_k, rows_v)
    arriving = (arriving_k, arriving_v)

    def columns(which, owner):
        return pools[which].at[:, :, pl.ds(pl.multiple_of(owner * WIDTH, WIDTH), WIDTH)]

    def tp_copy(which, step):
        peer = lax.rem(my_tp + step, N_TP)
        return pltpu.make_async_remote_copy(
            src_ref=columns(which, peer),
            dst_ref=rows[which].at[pl.ds(my_tp * 32, 32)],
            send_sem=tp_send.at[which, step],
            recv_sem=tp_recv.at[which, step],
            device_id={"tp": peer},
            device_id_type=MESH,
        )

    def own_copy(which):
        return pltpu.make_async_copy(
            columns(which, my_tp), rows[which].at[pl.ds(my_tp * 32, 32)], own_sem.at[which]
        )

    for which in range(2):
        for step in (1, 3, 2):
            tp_copy(which, step).start()
        own_copy(which).start()

    loads = [
        pltpu.make_async_copy(hidden, hidden_buf, load_sem.at[0]),
        pltpu.make_async_copy(w_key, w_buf.at[0], load_sem.at[1]),
        pltpu.make_async_copy(w_value, w_buf.at[1], load_sem.at[2]),
    ]
    for load in loads:
        load.start()

    my_passage = lax.rem(me, PASSAGES)
    my_start = recompute_blocks[my_passage, me // PASSAGES] * BLOCK
    q_cos, q_sin = rotation(offsets[my_passage] + my_start, BLOCK, rates[...])
    for head in range(HEADS):
        cols = slice(head * HD, (head + 1) * HD)
        turned[head] = turn(queries[:, cols].astype(jnp.float32), q_cos, q_sin).astype(jnp.bfloat16)
    group_z = z - half + lax.rem(half + y + core, 2)

    def q_dest(other_y):
        return group_z * 8 + other_y * 2 + core

    def q_remote(other_y):
        return on_seq(
            turned, out_q.at[y], q_send.at[other_y], q_recv.at[y], q_dest(other_y)
        )

    def q_local():
        return pltpu.make_async_copy(turned, out_q.at[y], q_recv.at[y])

    which_block = me // PASSAGES
    home = lax.rem(me, PASSAGES) * 2

    def f_remote(side):
        return on_seq(
            fresh, fresh_in.at[which_block], f_send.at[side], f_recv.at[which_block], home + side
        )

    def f_local():
        return pltpu.make_async_copy(fresh, fresh_in.at[which_block], f_recv.at[which_block])

    for other_y in range(4):

        @pl.when(q_dest(other_y) != me)
        def _():
            q_remote(other_y).start()

        @pl.when(q_dest(other_y) == me)
        def _():
            q_local().start()

    for row in range(PASSAGES):
        used[row : row + 1, :] = page_slot[pl.ds(passage_ids[row], 1), :]
    slots = used[...]
    lane = lax.broadcasted_iota(jnp.int32, slots.shape, 1)
    in_half = lax.rem(lane, PER_DEST)
    hit = (slots >> 7) == me
    rank = hit.astype(jnp.int32)
    for shift in (1, 2, 4, 8, 16, 32):
        rank = rank + jnp.where(in_half >= shift, pltpu.roll(rank, shift, 1), 0)
    table = jnp.zeros(slots.shape, jnp.int32)
    for side in range(2):
        for order in range(CAP):
            wanted = hit & (rank == order + 1) & ((lane >= PER_DEST) == (side == 1))
            local = jnp.where(wanted, slots & 127, 0)
            for shift in (64, 32, 16, 8, 4, 2, 1):
                local = local + pltpu.roll(local, shift, 1)
            table = jnp.where(lane == side * CAP + order, local, table)
    send_tab[...] = table
    source = jnp.broadcast_to(used[pl.ds(me // 2, 1), :], (8, HD)) >> 7
    lane = lax.broadcasted_iota(jnp.int32, source.shape, 1)
    in_half = lax.rem(lane, PER_DEST)
    rank = jnp.zeros(source.shape, jnp.int32)
    for shift in range(1, PER_DEST):
        same = (pltpu.roll(source, shift, 1) == source) & (in_half >= shift)
        rank = rank + same.astype(jnp.int32)
    arrival_tab[...] = source * CAP + rank
    index_copies = [
        pltpu.make_async_copy(send_tab, send_index, load_sem.at[3]),
        pltpu.make_async_copy(arrival_tab, arrival, load_sem.at[4]),
    ]
    for copy in index_copies:
        copy.start()

    for load in loads:
        load.wait()

    def multiply(part, totals):
        depth = pl.ds(pl.multiple_of(part * 1024, 1024), 1024)
        return tuple(
            total
            + jnp.dot(hidden_buf[:, depth], w_buf[which, depth, :], preferred_element_type=jnp.float32)
            for which, total in enumerate(totals)
        )

    nothing = jnp.zeros((BLOCK, WIDTH), jnp.float32)
    raw_k, raw_v = lax.fori_loop(0, 8, multiply, (nothing, nothing))
    for head in range(2):
        cols = slice(head * HD, (head + 1) * HD)
        fresh[0, :, cols] = turn(raw_k[:, cols], q_cos, q_sin).astype(jnp.bfloat16)
    fresh[1] = raw_v.astype(jnp.bfloat16)
    for side in range(2):

        @pl.when(home + side != me)
        def _():
            f_remote(side).start()

        @pl.when(home + side == me)
        def _():
            f_local().start()

    token_cos, token_sin = rotation(offsets[me // 2] + core * TOK_DEV, TOK_DEV, rates[...])
    t_cos[...] = token_cos
    t_sin[...] = token_sin
    for copy in index_copies:
        copy.wait()

    def page_copy(which, step):
        peer = lax.rem(me + step, N_SEQ)
        return on_seq(
            outgoing.at[which, peer],
            arriving[which].at[me],
            page_send.at[which, step],
            page_recv.at[which, step],
            peer,
        )

    for which in range(2):
        for step in range(1, N_TP):
            peer = lax.rem(my_tp + N_TP - step, N_TP)
            pltpu.make_async_remote_copy(
                src_ref=columns(which, my_tp),
                dst_ref=rows[which].at[pl.ds(peer * 32, 32)],
                send_sem=tp_send.at[which, step],
                recv_sem=tp_recv.at[which, step],
                device_id={"tp": peer},
                device_id_type=MESH,
            ).wait_recv()
        own_copy(which).wait()

        def pick(step, _):
            peer = lax.rem(me + step, N_SEQ)
            for rank in range(CAP):
                outgoing[which, peer, rank] = rows[which][
                    send_index[peer // 2, lax.rem(peer, 2) * CAP + rank]
                ]

            @pl.when(step > 0)
            def _():
                page_copy(which, step).start()

            return 0

        lax.fori_loop(0, N_SEQ, pick, 0)
        arriving[which][me] = outgoing[which, me]

    for slot in range(4):
        on_seq(turned, out_q.at[slot], q_send.at[0], q_recv.at[slot], me).wait_recv()
    for slot in range(2):
        on_seq(fresh, fresh_in.at[slot], f_send.at[0], f_recv.at[slot], me).wait_recv()

    for which in range(2):

        def landed(step, _):
            sender = lax.rem(me + N_SEQ - step, N_SEQ)
            on_seq(
                outgoing.at[which, me],
                arriving[which].at[sender],
                page_send.at[which, step],
                page_recv.at[which, step],
                sender,
            ).wait_recv()
            return 0

        lax.fori_loop(1, N_SEQ, landed, 0)

        def put(page, _):
            slot = arrival[0, core * PER_DEST + page]
            block = core * 8 + page // 8
            first, second = (recompute_blocks[me // 2, number] for number in range(RB))
            where = pl.ds(pl.multiple_of(page * PAGE, PAGE), PAGE)
            within = pl.ds(pl.multiple_of(lax.rem(page, 8) * PAGE, PAGE), PAGE)
            got = arriving[which][slot // CAP, lax.rem(slot, CAP)]
            if which == 0:
                wide = got.astype(jnp.float32)
                cosine, sine = t_cos[where], t_sin[where]
                got = jnp.concatenate(
                    [
                        turn(wide[:, :HD], cosine, sine).astype(jnp.bfloat16),
                        turn(wide[:, HD:], cosine, sine).astype(jnp.bfloat16),
                    ],
                    axis=1,
                )
            new = fresh_in[jnp.where(second == block, 1, 0), which, within]
            here = jnp.full(got.shape, block, jnp.int32)
            flag = (here == first) | (here == second)
            mixed = jnp.where(flag, new.astype(jnp.float32), got.astype(jnp.float32))
            (out_k, out_v)[which][where] = mixed.astype(jnp.bfloat16)
            return 0

        lax.fori_loop(0, PER_DEST, put, 0)

    for which in range(2):
        for step in range(1, N_TP):
            tp_copy(which, step).wait_send()

        def sent(step, _):
            page_copy(which, step).wait_send()
            return 0

        lax.fori_loop(1, N_SEQ, sent, 0)
    for other_y in range(4):

        @pl.when(q_dest(other_y) != me)
        def _():
            q_remote(other_y).wait_send()

    for side in range(2):

        @pl.when(home + side != me)
        def _():
            f_remote(side).wait_send()


def attend_kernel(
    recompute_blocks,
    own_k, own_v, q_ref,
    out_ref,
    k_buf, v_buf, acc, peak, part, stat, part_in, stat_in,
    own_sem, kv_send, kv_recv, side_send, side_recv, part_send, part_recv,
):
    me = lax.axis_index("seq")
    z, y, core, half = place(me)
    pair = z - half
    group = group_of(half, core)
    sibling = me + 1 - 2 * core
    barrier = pltpu.get_barrier_semaphore()

    def greet(step, _):
        pl.semaphore_signal(
            barrier, inc=1, device_id={"seq": lax.rem(me + step, N_SEQ)}, device_id_type=MESH
        )
        return 0

    lax.fori_loop(1, N_SEQ, greet, 0)
    pl.semaphore_wait(barrier, N_SEQ - 1)

    owns = (own_k, own_v)
    bufs = (k_buf, v_buf)

    def near(step):
        return lax.rem(z + step, 4)

    def at(level):
        return level * 8 + y * 2 + core

    def own_copy(which):
        return pltpu.make_async_copy(owns[which], bufs[which].at[z, core], own_sem.at[which])

    def kv_copy(which, step):
        return on_seq(
            owns[which], bufs[which].at[z, core], kv_send.at[which, step],
            kv_recv.at[which, step], at(near(step)),
        )

    def kv_landed(which, step):
        level = near(4 - step)
        return on_seq(
            owns[which], bufs[which].at[level, core], kv_send.at[which, step],
            kv_recv.at[which, step], at(level),
        )

    def side_copy(which, step, passed_on):
        level = near(4 - step)
        source = bufs[which].at[level, core] if passed_on else owns[which]
        return on_seq(
            source, bufs[which].at[level, core], side_send.at[which, step],
            side_recv.at[which, step], sibling,
        )

    def side_landed(which, step):
        level = near(4 - step)
        return on_seq(
            owns[which], bufs[which].at[level, 1 - core], side_send.at[which, step],
            side_recv.at[which, step], sibling,
        )

    def pass_on(which):
        level, ahead = (near(3), near(1)) if which == 0 else (near(1), near(3))
        return on_seq(
            bufs[which].at[level, core], bufs[which].at[level, core], kv_send.at[which, 2],
            kv_recv.at[which, 2], at(ahead),
        )

    for which in range(2):
        side_copy(which, 0, False).start()
        own_copy(which).start()
    for which, step in ((0, 1), (1, 3), (1, 1), (0, 3)):
        kv_copy(which, step).start()
    acc[...] = jnp.zeros_like(acc)
    peak[...] = jnp.full_like(peak, MASKED)

    ones = jnp.ones((PASSAGE_LEN, HD), jnp.bfloat16)

    def fold(slot, level, limit):
        for index in range(8 // UNIT):
            for kv in range(2):
                cols = slice(kv * HD, (kv + 1) * HD)
                heads = slice(kv * 8 + index * UNIT, kv * 8 + (index + 1) * UNIT)
                q = q_ref[slot, heads].reshape(QT, HD)
                keys = k_buf[level].reshape(PASSAGE_LEN, WIDTH)[:, cols]
                values = v_buf[level].reshape(PASSAGE_LEN, WIDTH)[:, cols]
                score = lax.dot_general(q, keys, BY_KEY, preferred_element_type=jnp.float32)
                if limit is not None:
                    token = lax.broadcasted_iota(jnp.int32, score.shape, 1)
                    row = lax.broadcasted_iota(jnp.int32, score.shape, 0) % BLOCK + limit
                    allowed = token <= row
                    score = jnp.where(allowed, score, MASKED)
                old = peak[slot, heads].reshape(QT, HD)
                new = jnp.maximum(old, jnp.max(score, axis=1, keepdims=True))
                keep = jnp.exp2((old - new) * EXPONENT)
                weight = jnp.exp2((score - new[:, :1]) * EXPONENT).astype(jnp.bfloat16)
                total = jnp.dot(
                    weight,
                    jnp.concatenate([values, ones], axis=1),
                    preferred_element_type=jnp.float32,
                )
                before = acc[slot, heads].reshape(QT, 2 * HD)
                acc[slot, heads] = (before * keep[:, :1] + total).reshape(UNIT, BLOCK, 2 * HD)
                peak[slot, heads] = new.reshape(UNIT, BLOCK, HD)

    def slot_passage(slot):
        return slot_half(group, slot) * 8 + 2 * slot + core

    def visit(slot, level):
        passage = level * 4 + y
        mine = slot_passage(slot)

        @pl.when(passage < mine)
        def _():
            fold(slot, level, None)

        @pl.when(passage == mine)
        def _():
            fold(slot, level, recompute_blocks[mine, z // 2] * BLOCK)

    def owner(slot):
        return (pair + slot_half(group, slot)) * 8 + slot * 2 + core

    def part_copies(slot):
        return (
            on_seq(part.at[slot], part_in.at[y], part_send.at[0, slot], part_recv.at[0, y],
                   owner(slot)),
            on_seq(stat.at[slot], stat_in.at[y], part_send.at[1, slot], part_recv.at[1, y],
                   owner(slot)),
        )

    def local_copies(slot):
        return (
            pltpu.make_async_copy(part.at[slot], part_in.at[y], part_recv.at[0, y]),
            pltpu.make_async_copy(stat.at[slot], stat_in.at[y], part_recv.at[1, y]),
        )

    def give_back(slot):
        lane = lax.broadcasted_iota(jnp.int32, (BLOCK, HD), 1)

        def head_part(head, logs):
            total = acc[slot, head]
            weight_sum = total[:, HD:]
            some = weight_sum > 0.0
            safe = jnp.where(some, weight_sum, 1.0)
            part[slot, head] = (total[:, :HD] / safe).astype(jnp.bfloat16)
            size = jnp.where(some, peak[slot, head] * EXPONENT + jnp.log2(safe), MASKED)
            return jnp.where(lane == head, size, logs)

        stat[slot] = lax.fori_loop(
            0, HEADS, head_part, jnp.full((BLOCK, HD), MASKED, jnp.float32)
        )

        @pl.when(owner(slot) != me)
        def _():
            for copy in part_copies(slot):
                copy.start()

        @pl.when(owner(slot) == me)
        def _():
            for copy in local_copies(slot):
                copy.start()

    def ranked(order):
        return 2 * lax.rem(order, 2) + lax.rem(order // 2 + group, 2)

    def arrive(turn_index, _):
        @pl.when(turn_index == 0)
        def _():
            for which in range(2):
                own_copy(which).wait()
                side_landed(which, 0).wait_recv()

        @pl.when(turn_index == 1)
        def _():
            kv_landed(1, 1).wait_recv()
            side_copy(1, 1, True).start()
            kv_landed(0, 3).wait_recv()
            side_copy(0, 3, True).start()
            for which in range(2):
                side_landed(which, 1).wait_recv()

        @pl.when(turn_index == 2)
        def _():
            for which in range(2):
                kv_landed(which, 2).wait_recv()
                side_copy(which, 2, True).start()
                side_landed(which, 3).wait_recv()
            for which in range(2):
                side_landed(which, 2).wait_recv()

        def each(order, _):
            slot = ranked(jnp.where(turn_index == 2, order // 2, 3 - order))
            step = jnp.where(turn_index == 2, 3 - lax.rem(order, 2), turn_index)
            visit(slot, near(4 - step))

            @pl.when((turn_index == 0) & (order == 1))
            def _():
                for which, early_step in ((0, 1), (1, 3)):
                    kv_landed(which, early_step).wait_recv()
                    pass_on(which).start()
                    side_copy(which, early_step, True).start()

            @pl.when((turn_index == 2) & (lax.rem(order, 2) == 1))
            def _():
                give_back(slot)

            return 0

        lax.fori_loop(0, jnp.where(turn_index == 2, 8, 4), each, 0)
        return 0

    lax.fori_loop(0, 3, arrive, 0)

    for slot in range(4):
        on_seq(part.at[0], part_in.at[slot], part_send.at[0, 0], part_recv.at[0, slot],
               me).wait_recv()
        on_seq(stat.at[0], stat_in.at[slot], part_send.at[1, 0], part_recv.at[1, slot],
               me).wait_recv()
    logs = [stat_in[slot] for slot in range(4)]
    top = jnp.maximum(jnp.maximum(logs[0], logs[1]), jnp.maximum(logs[2], logs[3]))
    shares = [jnp.exp2(log - top) for log in logs]
    whole = 1.0 / (shares[0] + shares[1] + shares[2] + shares[3])
    shares = [share * whole for share in shares]
    for head in range(HEADS):
        result = sum(
            part_in[slot, head].astype(jnp.float32) * shares[slot][:, head : head + 1]
            for slot in range(4)
        )
        out_ref[:, head * HD : (head + 1) * HD] = result.astype(jnp.bfloat16)

    for which in range(2):
        for step in (1, 3):
            kv_copy(which, step).wait_send()
        pass_on(which).wait_send()
        for step in range(4):
            side_copy(which, step, step > 0).wait_send()
    for slot in range(4):

        @pl.when(owner(slot) != me)
        def _():
            for copy in part_copies(slot):
                copy.wait_send()


def on_device(
    pool_keys,
    pool_values,
    passage_ids,
    page_slot,
    offsets,
    recompute_blocks,
    hidden_rows,
    w_key,
    w_value,
    queries,
):
    rates = frequencies()
    rates = jnp.concatenate([rates, rates])[None, :]
    vmem = pl.BlockSpec(memory_space=pltpu.VMEM)
    smem = pl.BlockSpec(memory_space=pltpu.SMEM)
    hbm = pl.BlockSpec(memory_space=pl.ANY)
    bf16 = jnp.bfloat16
    dma = pltpu.SemaphoreType.DMA
    key_cache, value_cache, q_group = pl.pallas_call(
        exchange_kernel,
        out_shape=[
            jax.ShapeDtypeStruct((TOK_DEV, WIDTH), bf16),
            jax.ShapeDtypeStruct((TOK_DEV, WIDTH), bf16),
            jax.ShapeDtypeStruct((4, HEADS, BLOCK, HD), bf16),
        ],
        in_specs=[smem, vmem, smem, smem, vmem, hbm, hbm, hbm, hbm, hbm, vmem],
        out_specs=[vmem, vmem, hbm],
        scratch_shapes=[
            pltpu.VMEM((128, PAGE, WIDTH), bf16),
            pltpu.VMEM((128, PAGE, WIDTH), bf16),
            pltpu.VMEM((2, N_SEQ, CAP, PAGE, WIDTH), bf16),
            pltpu.VMEM((N_SEQ, CAP, PAGE, WIDTH), bf16),
            pltpu.VMEM((N_SEQ, CAP, PAGE, WIDTH), bf16),
            pltpu.VMEM((HEADS, BLOCK, HD), bf16),
            pltpu.VMEM((2, BLOCK, WIDTH), bf16),
            pltpu.VMEM((RB, 2, BLOCK, WIDTH), bf16),
            pltpu.VMEM((BLOCK, 8192), bf16),
            pltpu.VMEM((2, 8192, WIDTH), bf16),
            pltpu.VMEM((TOK_DEV, HD), jnp.float32),
            pltpu.VMEM((TOK_DEV, HD), jnp.float32),
            pltpu.VMEM((PASSAGES, HD), jnp.int32),
            pltpu.VMEM((PASSAGES, HD), jnp.int32),
            pltpu.VMEM((8, HD), jnp.int32),
            pltpu.SMEM((PASSAGES, HD), jnp.int32),
            pltpu.SMEM((8, HD), jnp.int32),
            dma((2,)),
            dma((5,)),
            dma((2, N_TP)),
            dma((2, N_TP)),
            dma((2, N_SEQ)),
            dma((2, N_SEQ)),
            dma((4,)),
            dma((4,)),
            dma((2,)),
            dma((2,)),
        ],
        compiler_params=pltpu.CompilerParams(
            collective_id=0, has_side_effects=True, vmem_limit_bytes=48 * 2**20
        ),
        name="exchange",
    )(
        passage_ids, page_slot, offsets, recompute_blocks, rates,
        pool_keys, pool_values, hidden_rows, w_key, w_value, queries,
    )

    attended = pl.pallas_call(
        attend_kernel,
        out_shape=jax.ShapeDtypeStruct((BLOCK, HEADS * HD), bf16),
        in_specs=[smem, hbm, hbm, vmem],
        out_specs=vmem,
        scratch_shapes=[
            pltpu.VMEM((4, 2, TOK_DEV, WIDTH), bf16),
            pltpu.VMEM((4, 2, TOK_DEV, WIDTH), bf16),
            pltpu.VMEM((4, HEADS, BLOCK, 2 * HD), jnp.float32),
            pltpu.VMEM((4, HEADS, BLOCK, HD), jnp.float32),
            pltpu.VMEM((4, HEADS, BLOCK, HD), bf16),
            pltpu.VMEM((4, BLOCK, HD), jnp.float32),
            pltpu.VMEM((4, HEADS, BLOCK, HD), bf16),
            pltpu.VMEM((4, BLOCK, HD), jnp.float32),
            dma((2,)),
            dma((2, 4)),
            dma((2, 4)),
            dma((2, 4)),
            dma((2, 4)),
            dma((2, 4)),
            dma((2, 4)),
        ],
        compiler_params=pltpu.CompilerParams(
            collective_id=1, has_side_effects=True, vmem_limit_bytes=56 * 2**20
        ),
        name="attend",
    )(recompute_blocks, key_cache, value_cache, q_group)
    return (key_cache, value_cache, attended)


def solution(mesh):
    placed = (
        P(("seq", "tp"), None, None),
        P(("seq", "tp"), None, None),
        P(),
        P(),
        P(),
        P(),
        P("seq", None),
        P(None, "tp"),
        P(None, "tp"),
        P("seq", "tp"),
    )
    return jax.shard_map(
        on_device,
        mesh=mesh,
        in_specs=placed,
        out_specs=(P("seq", "tp"), P("seq", "tp"), P("seq", "tp")),
        check_vma=False,
    )
```

```python
import math

import jax
import jax.numpy as jnp
import numpy as np
from jax import lax
from jax.experimental import pallas as pl
from jax.experimental.pallas import tpu as pltpu
from jax.sharding import PartitionSpec as P

HD = 128
PASSAGE_LEN = 2048
BLOCK = 128
PAGE = 16
RB = 2
TOK_DEV = 1024
CAP = 4
N_SEQ = 32
N_TP = 4
PASSAGES = 16
PER_DEST = TOK_DEV // PAGE
WIDTH = 256
HEADS = 16
MASKED = -1e30
EXPONENT = math.log2(math.e) / math.sqrt(HD)
QT = 256
UNIT = QT // BLOCK
BY_KEY = (((1,), (1,)), ((), ()))
MESH = pl.DeviceIdType.MESH


def frequencies():
    base_rate = 500000.0 ** (-np.arange(0, HD, 2) / HD)
    wave_length = 2.0 * math.pi / base_rate
    smooth = (8192.0 / wave_length - 1.0) / 3.0
    blended = (1.0 - smooth) * base_rate / 8.0 + smooth * base_rate
    rates = np.where(
        wave_length > 8192.0, base_rate / 8.0, np.where(wave_length < 2048.0, base_rate, blended)
    )
    return np.concatenate([rates, rates])[None, :].astype(np.float32)


def turn(values, cosine, sine):
    return values * cosine + pltpu.roll(values, HD // 2, 1) * sine


def on_seq(source, target, send_sem, recv_sem, peer):
    return pltpu.make_async_remote_copy(
        src_ref=source,
        dst_ref=target,
        send_sem=send_sem,
        recv_sem=recv_sem,
        device_id={"seq": peer},
        device_id_type=MESH,
    )


def place(me):
    z = me // 8
    return z, (me // 2) % 4, me % 2, z % 2


def home_level(z, core, slot):
    return lax.rem(z + lax.rem(core + slot, 2) * (3 - 2 * (slot // 2)), 4)


def group_home(z, core, y):
    return lax.rem(z + lax.rem(core + y, 2) * (1 + 2 * (y // 2)), 4)


def rotation(first, count, rates):
    places = lax.broadcasted_iota(jnp.int32, (count, HD), 0) + first
    angles = places.astype(jnp.float32) * rates
    sine = jnp.sin(angles)
    lane = lax.broadcasted_iota(jnp.int32, (count, HD), 1)
    return jnp.cos(angles), jnp.where(lane < HD // 2, -sine, sine)


def blend_kernel(
    passage_ids, page_slot, offsets, recompute_blocks, rates,
    pool_k, pool_v, hidden, w_key, w_value, queries,
    out_k, out_v, out_ref,
    query_buf, slot_buf, q_group, rows_k, rows_v, outgoing, arriving_k, arriving_v, turned, fresh, fresh_in,
    hidden_buf, w_buf, t_cos, t_sin, used, send_tab, arrival_tab, send_index, arrival,
    k_buf, v_buf, acc, peak, part, stat, part_in, stat_in,
    own_sem, load_sem, tp_send, tp_recv, page_send, page_recv, q_send, q_recv, f_send, f_recv,
    out_sem, kv_send, kv_recv, side_send, side_recv, part_send, part_recv,
):
    me = lax.axis_index("seq")
    my_tp = lax.axis_index("tp")
    z, y, core, half = place(me)
    barrier = pltpu.get_barrier_semaphore()

    def greet_seq(step, _):
        pl.semaphore_signal(
            barrier, inc=1, device_id={"seq": lax.rem(me + step, N_SEQ)}, device_id_type=MESH
        )
        return 0

    lax.fori_loop(1, N_SEQ, greet_seq, 0)
    for step in range(1, N_TP):
        pl.semaphore_signal(
            barrier, inc=1, device_id={"tp": lax.rem(my_tp + step, N_TP)}, device_id_type=MESH
        )

    loads = [
        pltpu.make_async_copy(hidden, hidden_buf, load_sem.at[0]),
        pltpu.make_async_copy(w_key, w_buf.at[0], load_sem.at[1]),
        pltpu.make_async_copy(w_value, w_buf.at[1], load_sem.at[2]),
        pltpu.make_async_copy(queries, query_buf, load_sem.at[5]),
        pltpu.make_async_copy(page_slot, slot_buf, load_sem.at[6]),
    ]
    for load in loads:
        load.start()

    loads[3].wait()
    my_passage = lax.rem(me, PASSAGES)
    my_start = recompute_blocks[my_passage * RB + me // PASSAGES] * BLOCK
    q_cos, q_sin = rotation(offsets[my_passage] + my_start, BLOCK, rates[...])
    for head in range(HEADS):
        cols = slice(head * HD, (head + 1) * HD)
        turned[head] = turn(query_buf[:, cols].astype(jnp.float32), q_cos, q_sin).astype(jnp.bfloat16)
    acc[...] = jnp.zeros_like(acc)
    peak[...] = jnp.full_like(peak, MASKED)
    pl.semaphore_wait(barrier, N_SEQ - 1 + N_TP - 1)

    group = lax.rem(half + core, 2)
    sibling = me + 1 - 2 * core
    bufs = (k_buf, v_buf)

    def near(step):
        return lax.rem(z + step, 4)

    def at(level):
        return level * 8 + y * 2 + core

    def keep_copy(which):
        return pltpu.make_async_copy(
            bufs[which].at[z, core], (out_k, out_v)[which], out_sem.at[which]
        )

    def kv_copy(which, step):
        return on_seq(
            bufs[which].at[z, core], bufs[which].at[z, core], kv_send.at[which, step],
            kv_recv.at[which, step], at(near(step)),
        )

    def kv_landed(which, step):
        level = near(4 - step)
        return on_seq(
            bufs[which].at[z, core], bufs[which].at[level, core], kv_send.at[which, step],
            kv_recv.at[which, step], at(level),
        )

    def side_copy(which, step):
        level = near(4 - step)
        return on_seq(
            bufs[which].at[level, core], bufs[which].at[level, core], side_send.at[which, step],
            side_recv.at[which, step], sibling,
        )

    def side_landed(which, step):
        level = near(4 - step)
        return on_seq(
            bufs[which].at[z, core], bufs[which].at[level, 1 - core], side_send.at[which, step],
            side_recv.at[which, step], sibling,
        )

    def pass_on(which):
        level, ahead = (near(3), near(1)) if which == 0 else (near(1), near(3))
        return on_seq(
            bufs[which].at[level, core], bufs[which].at[level, core], kv_send.at[which, 2],
            kv_recv.at[which, 2], at(ahead),
        )

    pools = (pool_k, pool_v)
    rows = (rows_k, rows_v)
    arriving = (arriving_k, arriving_v)

    def columns(which, owner):
        return pools[which].at[:, :, pl.ds(pl.multiple_of(owner * WIDTH, WIDTH), WIDTH)]

    def tp_copy(which, step):
        peer = lax.rem(my_tp + step, N_TP)
        return pltpu.make_async_remote_copy(
            src_ref=columns(which, peer),
            dst_ref=rows[which].at[pl.ds(my_tp * 32, 32)],
            send_sem=tp_send.at[which, step],
            recv_sem=tp_recv.at[which, step],
            device_id={"tp": peer},
            device_id_type=MESH,
        )

    def own_copy(which):
        return pltpu.make_async_copy(
            columns(which, my_tp), rows[which].at[pl.ds(my_tp * 32, 32)], own_sem.at[which]
        )

    def tp_start(which):
        for step in (1, 3, 2):
            tp_copy(which, step).start()
        own_copy(which).start()

    tp_start(0)

    group_z = group_home(z, core, y)

    def q_dest(other_y):
        return group_z * 8 + other_y * 2 + core

    def q_remote(other_y):
        return on_seq(
            turned, q_group.at[y], q_send.at[other_y], q_recv.at[y], q_dest(other_y)
        )

    def q_local():
        return pltpu.make_async_copy(turned, q_group.at[y], q_recv.at[y])

    which_block = me // PASSAGES
    home = lax.rem(me, PASSAGES) * 2

    def f_remote(side):
        return on_seq(
            fresh, fresh_in.at[which_block], f_send.at[side], f_recv.at[which_block], home + side
        )

    def f_local():
        return pltpu.make_async_copy(fresh, fresh_in.at[which_block], f_recv.at[which_block])

    for other_y in range(4):

        @pl.when(q_dest(other_y) != me)
        def _():
            q_remote(other_y).start()

        @pl.when(q_dest(other_y) == me)
        def _():
            q_local().start()

    loads[4].wait()
    for row in range(PASSAGES):
        used[row : row + 1, :] = slot_buf[pl.ds(passage_ids[row], 1), :]
    slots = used[...]
    lane = lax.broadcasted_iota(jnp.int32, slots.shape, 1)
    in_half = lax.rem(lane, PER_DEST)
    hit = (slots >> 7) == me
    rank = hit.astype(jnp.int32)
    for shift in (1, 2, 4, 8, 16, 32):
        rank = rank + jnp.where(in_half >= shift, pltpu.roll(rank, shift, 1), 0)
    table = jnp.zeros(slots.shape, jnp.int32)
    for side in range(2):
        for order in range(CAP):
            wanted = hit & (rank == order + 1) & ((lane >= PER_DEST) == (side == 1))
            local = jnp.where(wanted, slots & 127, 0)
            for shift in (64, 32, 16, 8, 4, 2, 1):
                local = local + pltpu.roll(local, shift, 1)
            table = jnp.where(lane == side * CAP + order, local, table)
    send_tab[...] = table
    source = jnp.broadcast_to(used[pl.ds(me // 2, 1), :], (8, HD)) >> 7
    lane = lax.broadcasted_iota(jnp.int32, source.shape, 1)
    in_half = lax.rem(lane, PER_DEST)
    rank = jnp.zeros(source.shape, jnp.int32)
    for shift in range(1, PER_DEST):
        same = (pltpu.roll(source, shift, 1) == source) & (in_half >= shift)
        rank = rank + same.astype(jnp.int32)
    arrival_tab[...] = source * CAP + rank
    index_copies = [
        pltpu.make_async_copy(send_tab, send_index, load_sem.at[3]),
        pltpu.make_async_copy(arrival_tab, arrival, load_sem.at[4]),
    ]
    for copy in index_copies:
        copy.start()


    for load in loads[:3]:
        load.wait()

    def multiply(part, totals):
        depth = pl.ds(pl.multiple_of(part * 1024, 1024), 1024)
        return tuple(
            total
            + jnp.dot(hidden_buf[:, depth], w_buf[which, depth, :], preferred_element_type=jnp.float32)
            for which, total in enumerate(totals)
        )

    nothing = jnp.zeros((BLOCK, WIDTH), jnp.float32)
    raw_k, raw_v = lax.fori_loop(0, 8, multiply, (nothing, nothing))
    for head in range(2):
        cols = slice(head * HD, (head + 1) * HD)
        fresh[0, :, cols] = turn(raw_k[:, cols], q_cos, q_sin).astype(jnp.bfloat16)
    fresh[1] = raw_v.astype(jnp.bfloat16)
    for side in range(2):

        @pl.when(home + side != me)
        def _():
            f_remote(side).start()

        @pl.when(home + side == me)
        def _():
            f_local().start()

    token_cos, token_sin = rotation(offsets[me // 2] + core * TOK_DEV, TOK_DEV, rates[...])
    t_cos[...] = token_cos
    t_sin[...] = token_sin
    for copy in index_copies:
        copy.wait()

    def page_copy(which, step):
        peer = lax.rem(me + step, N_SEQ)
        return on_seq(
            outgoing.at[which, peer],
            arriving[which].at[me],
            page_send.at[which, step],
            page_recv.at[which, step],
            peer,
        )

    for which in range(2):
        for step in range(1, N_TP):
            peer = lax.rem(my_tp + N_TP - step, N_TP)
            pltpu.make_async_remote_copy(
                src_ref=columns(which, my_tp),
                dst_ref=rows[which].at[pl.ds(peer * 32, 32)],
                send_sem=tp_send.at[which, step],
                recv_sem=tp_recv.at[which, step],
                device_id={"tp": peer},
                device_id_type=MESH,
            ).wait_recv()
        own_copy(which).wait()
        if which == 0:
            tp_start(1)

        def pick(step, _):
            peer = lax.rem(me + step, N_SEQ)
            for rank in range(CAP):
                outgoing[which, peer, rank] = rows[which][
                    send_index[peer // 2, lax.rem(peer, 2) * CAP + rank]
                ]

            @pl.when(step > 0)
            def _():
                page_copy(which, step).start()

            return 0

        lax.fori_loop(0, N_SEQ, pick, 0)
        arriving[which][me] = outgoing[which, me]

    for slot in range(4):
        on_seq(turned, q_group.at[slot], q_send.at[0], q_recv.at[slot], me).wait_recv()
    for slot in range(2):
        on_seq(fresh, fresh_in.at[slot], f_send.at[0], f_recv.at[slot], me).wait_recv()

    for which in range(2):

        def landed(step, _):
            sender = lax.rem(me + N_SEQ - step, N_SEQ)
            on_seq(
                outgoing.at[which, me],
                arriving[which].at[sender],
                page_send.at[which, step],
                page_recv.at[which, step],
                sender,
            ).wait_recv()
            return 0

        lax.fori_loop(1, N_SEQ, landed, 0)

        def put(index, _):
            block = core * 8 + index
            first, second = (recompute_blocks[me // 2 * RB + number] for number in range(RB))
            here = jnp.full((PAGE, WIDTH), block, jnp.int32)
            flag = (here == first) | (here == second)
            for page in range(8):
                slot = arrival[0, core * PER_DEST + index * 8 + page]
                where = pl.ds(pl.multiple_of(index * BLOCK + page * PAGE, PAGE), PAGE)
                got = arriving[which][slot // CAP, lax.rem(slot, CAP)].astype(jnp.float32)
                if which == 0:
                    cosine, sine = t_cos[where], t_sin[where]
                    got = jnp.concatenate(
                        [turn(got[:, :HD], cosine, sine), turn(got[:, HD:], cosine, sine)], axis=1
                    )
                within = slice(page * PAGE, (page + 1) * PAGE)
                new = fresh_in[jnp.where(second == block, 1, 0), which, within]
                mixed = jnp.where(flag, new.astype(jnp.float32), got)
                bufs[which][z, core, where] = mixed.astype(jnp.bfloat16)
            return 0

        lax.fori_loop(0, 8, put, 0)
        keep_copy(which).start()
        side_copy(which, 0).start()
        for step in (1, 3):
            kv_copy(which, step).start()

    ones = jnp.ones((PASSAGE_LEN, HD), jnp.bfloat16)

    def fold(slot, level, limit):
        for index in range(8 // UNIT):
            for kv in range(2):
                cols = slice(kv * HD, (kv + 1) * HD)
                heads = slice(kv * 8 + index * UNIT, kv * 8 + (index + 1) * UNIT)
                q = q_group[slot, heads].reshape(QT, HD)
                keys = k_buf[level].reshape(PASSAGE_LEN, WIDTH)[:, cols]
                values = v_buf[level].reshape(PASSAGE_LEN, WIDTH)[:, cols]
                score = lax.dot_general(q, keys, BY_KEY, preferred_element_type=jnp.float32)
                if limit is not None:
                    token = lax.broadcasted_iota(jnp.int32, score.shape, 1)
                    row = lax.broadcasted_iota(jnp.int32, score.shape, 0) % BLOCK + limit
                    allowed = token <= row
                    score = jnp.where(allowed, score, MASKED)
                old = peak[slot, heads].reshape(QT, HD)
                new = jnp.maximum(old, jnp.max(score, axis=1, keepdims=True))
                keep = jnp.exp2((old - new) * EXPONENT)
                weight = jnp.exp2((score - new[:, :1]) * EXPONENT).astype(jnp.bfloat16)
                total = jnp.dot(
                    weight,
                    jnp.concatenate([values, ones], axis=1),
                    preferred_element_type=jnp.float32,
                )
                before = acc[slot, heads].reshape(QT, 2 * HD)
                acc[slot, heads] = (before * keep[:, :1] + total).reshape(UNIT, BLOCK, 2 * HD)
                peak[slot, heads] = new.reshape(UNIT, BLOCK, HD)

    def slot_passage(slot):
        return lax.rem(group + slot, 2) * 8 + 2 * slot + core

    def visit(slot, level):
        passage = level * 4 + y
        mine = slot_passage(slot)

        @pl.when(passage < mine)
        def _():
            fold(slot, level, None)

        @pl.when(passage == mine)
        def _():
            fold(slot, level, recompute_blocks[mine * RB + home_level(z, core, slot) // 2] * BLOCK)

    def owner(slot):
        return home_level(z, core, slot) * 8 + slot * 2 + core

    def part_copies(slot):
        return (
            on_seq(part.at[slot], part_in.at[y], part_send.at[0, slot], part_recv.at[0, y],
                   owner(slot)),
            on_seq(stat.at[slot], stat_in.at[y], part_send.at[1, slot], part_recv.at[1, y],
                   owner(slot)),
        )

    def local_copies(slot):
        return (
            pltpu.make_async_copy(part.at[slot], part_in.at[y], part_recv.at[0, y]),
            pltpu.make_async_copy(stat.at[slot], stat_in.at[y], part_recv.at[1, y]),
        )

    def give_back(slot):
        lane = lax.broadcasted_iota(jnp.int32, (BLOCK, HD), 1)

        def head_part(head, logs):
            total = acc[slot, head]
            weight_sum = total[:, HD:]
            some = weight_sum > 0.0
            safe = jnp.where(some, weight_sum, 1.0)
            part[slot, head] = (total[:, :HD] / safe).astype(jnp.bfloat16)
            size = jnp.where(some, peak[slot, head] * EXPONENT + jnp.log2(safe), MASKED)
            return jnp.where(lane == head, size, logs)

        stat[slot] = lax.fori_loop(
            0, HEADS, head_part, jnp.full((BLOCK, HD), MASKED, jnp.float32), unroll=4
        )

        @pl.when(owner(slot) != me)
        def _():
            for copy in part_copies(slot):
                copy.start()

        @pl.when(owner(slot) == me)
        def _():
            for copy in local_copies(slot):
                copy.start()

    def ranked(order):
        return 2 * lax.rem(order, 2) + lax.rem(order // 2 + group, 2)

    def arrive(turn_index, _):
        @pl.when(turn_index == 0)
        def _():
            for which in range(2):
                side_landed(which, 0).wait_recv()

        @pl.when(turn_index == 1)
        def _():
            kv_landed(1, 1).wait_recv()
            side_copy(1, 1).start()
            kv_landed(0, 3).wait_recv()
            side_copy(0, 3).start()
            for which in range(2):
                side_landed(which, 1).wait_recv()

        @pl.when(turn_index == 2)
        def _():
            for which in range(2):
                side_landed(which, 3).wait_recv()

        step = jnp.where(turn_index < 2, turn_index, 5 - turn_index)
        level = near(4 - step)

        @pl.when(turn_index == 3)
        def _():
            def early(order, _):
                slot = ranked(order)

                @pl.when(slot_passage(slot) < level * 4 + y)
                def _():
                    give_back(slot)

                return 0

            lax.fori_loop(0, 4, early, 0)
            for which in range(2):
                kv_landed(which, 2).wait_recv()
                side_copy(which, 2).start()
            for which in range(2):
                side_landed(which, 2).wait_recv()

        def each(order, _):
            slot = ranked(jnp.where(turn_index == 3, order, 3 - order))
            visit(slot, level)

            @pl.when((turn_index == 0) & (order == 1))
            def _():
                for which, early_step in ((0, 1), (1, 3)):
                    kv_landed(which, early_step).wait_recv()
                    pass_on(which).start()
                    side_copy(which, early_step).start()

            @pl.when((turn_index == 3) & (slot_passage(slot) >= level * 4 + y))
            def _():
                give_back(slot)

            return 0

        lax.fori_loop(0, 4, each, 0)
        return 0

    lax.fori_loop(0, 4, arrive, 0)

    for slot in range(4):
        on_seq(part.at[0], part_in.at[slot], part_send.at[0, 0], part_recv.at[0, slot],
               me).wait_recv()
        on_seq(stat.at[0], stat_in.at[slot], part_send.at[1, 0], part_recv.at[1, slot],
               me).wait_recv()
    logs = [stat_in[slot] for slot in range(4)]
    top = jnp.maximum(jnp.maximum(logs[0], logs[1]), jnp.maximum(logs[2], logs[3]))
    shares = [jnp.exp2(log - top) for log in logs]
    whole = 1.0 / (shares[0] + shares[1] + shares[2] + shares[3])
    shares = [share * whole for share in shares]
    for head in range(HEADS):
        result = sum(
            part_in[slot, head].astype(jnp.float32) * shares[slot][:, head : head + 1]
            for slot in range(4)
        )
        out_ref[:, head * HD : (head + 1) * HD] = result.astype(jnp.bfloat16)

    for which in range(2):
        for step in (1, 3):
            kv_copy(which, step).wait_send()
        pass_on(which).wait_send()
        for step in range(4):
            side_copy(which, step).wait_send()
    for slot in range(4):

        @pl.when(owner(slot) != me)
        def _():
            for copy in part_copies(slot):
                copy.wait_send()
    for which in range(2):
        keep_copy(which).wait()
    for which in range(2):
        for step in range(1, N_TP):
            tp_copy(which, step).wait_send()

        def sent(step, _):
            page_copy(which, step).wait_send()
            return 0

        lax.fori_loop(1, N_SEQ, sent, 0)
    for other_y in range(4):

        @pl.when(q_dest(other_y) != me)
        def _():
            q_remote(other_y).wait_send()

    for side in range(2):

        @pl.when(home + side != me)
        def _():
            f_remote(side).wait_send()


def hand_out_kernel(key_in, value_in, attended_in, key_out, value_out, attended_out):
    key_out[...] = key_in[...]
    value_out[...] = value_in[...]
    attended_out[...] = attended_in[...]


def on_device(
    pool_keys,
    pool_values,
    passage_ids,
    page_slot,
    offsets,
    recompute_blocks,
    hidden_rows,
    w_key,
    w_value,
    queries,
):
    rates = jnp.asarray(frequencies())
    vmem = pl.BlockSpec(memory_space=pltpu.VMEM)
    smem = pl.BlockSpec(memory_space=pltpu.SMEM)
    hbm = pl.BlockSpec(memory_space=pltpu.HBM)
    bf16 = jnp.bfloat16
    dma = pltpu.SemaphoreType.DMA
    results = [
        jax.ShapeDtypeStruct((TOK_DEV, WIDTH), bf16),
        jax.ShapeDtypeStruct((TOK_DEV, WIDTH), bf16),
        jax.ShapeDtypeStruct((BLOCK, HEADS * HD), bf16),
    ]
    made = pl.pallas_call(
        blend_kernel,
        out_shape=results,
        in_specs=[smem, hbm, smem, smem, vmem, hbm, hbm, hbm, hbm, hbm, hbm],
        out_specs=[hbm, hbm, vmem],
        scratch_shapes=[
            pltpu.VMEM((BLOCK, HEADS * HD), bf16),
            pltpu.VMEM((32, HD), jnp.int32),
            pltpu.VMEM((4, HEADS, BLOCK, HD), bf16),
            pltpu.VMEM((128, PAGE, WIDTH), bf16),
            pltpu.VMEM((128, PAGE, WIDTH), bf16),
            pltpu.VMEM((2, N_SEQ, CAP, PAGE, WIDTH), bf16),
            pltpu.VMEM((N_SEQ, CAP, PAGE, WIDTH), bf16),
            pltpu.VMEM((N_SEQ, CAP, PAGE, WIDTH), bf16),
            pltpu.VMEM((HEADS, BLOCK, HD), bf16),
            pltpu.VMEM((2, BLOCK, WIDTH), bf16),
            pltpu.VMEM((RB, 2, BLOCK, WIDTH), bf16),
            pltpu.VMEM((BLOCK, 8192), bf16),
            pltpu.VMEM((2, 8192, WIDTH), bf16),
            pltpu.VMEM((TOK_DEV, HD), jnp.float32),
            pltpu.VMEM((TOK_DEV, HD), jnp.float32),
            pltpu.VMEM((PASSAGES, HD), jnp.int32),
            pltpu.VMEM((PASSAGES, HD), jnp.int32),
            pltpu.VMEM((8, HD), jnp.int32),
            pltpu.SMEM((PASSAGES, HD), jnp.int32),
            pltpu.SMEM((8, HD), jnp.int32),
            pltpu.VMEM((4, 2, TOK_DEV, WIDTH), bf16),
            pltpu.VMEM((4, 2, TOK_DEV, WIDTH), bf16),
            pltpu.VMEM((4, HEADS, BLOCK, 2 * HD), jnp.float32),
            pltpu.VMEM((4, HEADS, BLOCK, HD), jnp.float32),
            pltpu.VMEM((4, HEADS, BLOCK, HD), bf16),
            pltpu.VMEM((4, BLOCK, HD), jnp.float32),
            pltpu.VMEM((4, HEADS, BLOCK, HD), bf16),
            pltpu.VMEM((4, BLOCK, HD), jnp.float32),
            dma((2,)),
            dma((7,)),
            dma((2, N_TP)),
            dma((2, N_TP)),
            dma((2, N_SEQ)),
            dma((2, N_SEQ)),
            dma((4,)),
            dma((4,)),
            dma((2,)),
            dma((2,)),
            dma((2,)),
            dma((2, 4)),
            dma((2, 4)),
            dma((2, 4)),
            dma((2, 4)),
            dma((2, 4)),
            dma((2, 4)),
        ],
        compiler_params=pltpu.CompilerParams(
            collective_id=0, has_side_effects=True, vmem_limit_bytes=60 * 2**20
        ),
        name="blend_and_attend",
    )(
        passage_ids, page_slot, offsets, recompute_blocks.reshape(-1), rates,
        pool_keys, pool_values, hidden_rows, w_key, w_value, queries,
    )
    slabs = [pl.BlockSpec((r.shape[0] // 2, r.shape[1]), lambda i: (i, 0)) for r in results]
    return tuple(
        pl.pallas_call(
            hand_out_kernel,
            out_shape=results,
            grid=(2,),
            in_specs=slabs,
            out_specs=slabs,
            name="hand_out",
        )(*made)
    )


def solution(mesh):
    placed = (
        P(("seq", "tp"), None, None),
        P(("seq", "tp"), None, None),
        P(),
        P(),
        P(),
        P(),
        P("seq", None),
        P(None, "tp"),
        P(None, "tp"),
        P("seq", "tp"),
    )
    return jax.shard_map(
        on_device,
        mesh=mesh,
        in_specs=placed,
        out_specs=(P("seq", "tp"), P("seq", "tp"), P("seq", "tp")),
        check_vma=False,
    )
```

```python
import math

import jax
import jax.numpy as jnp
import numpy as np
from jax import lax
from jax.experimental import pallas as pl
from jax.experimental.pallas import tpu as pltpu
from jax.sharding import PartitionSpec as P

HD = 128
PASSAGE_LEN = 2048
BLOCK = 128
PAGE = 16
RB = 2
TOK_DEV = 1024
CAP = 4
N_SEQ = 32
N_TP = 4
PASSAGES = 16
PER_DEST = TOK_DEV // PAGE
WIDTH = 256
HEADS = 16
MASKED = -1e30
EXPONENT = math.log2(math.e) / math.sqrt(HD)
QT = 256
UNIT = QT // BLOCK
BY_KEY = (((1,), (1,)), ((), ()))
MESH = pl.DeviceIdType.MESH


def frequencies():
    base_rate = 500000.0 ** (-np.arange(0, HD, 2) / HD)
    wave_length = 2.0 * math.pi / base_rate
    smooth = (8192.0 / wave_length - 1.0) / 3.0
    blended = (1.0 - smooth) * base_rate / 8.0 + smooth * base_rate
    rates = np.where(
        wave_length > 8192.0, base_rate / 8.0, np.where(wave_length < 2048.0, base_rate, blended)
    )
    return np.concatenate([rates, rates])[None, :].astype(np.float32)


def turn(values, cosine, sine):
    return values * cosine + pltpu.roll(values, HD // 2, 1) * sine


def on_seq(source, target, send_sem, recv_sem, peer):
    return pltpu.make_async_remote_copy(
        src_ref=source,
        dst_ref=target,
        send_sem=send_sem,
        recv_sem=recv_sem,
        device_id={"seq": peer},
        device_id_type=MESH,
    )


def place(me):
    z = me // 8
    return z, (me // 2) % 4, me % 2, z % 2


def home_level(z, core, slot):
    return lax.rem(z + lax.rem(core + slot, 2) * (3 - 2 * (slot // 2)), 4)


def group_home(z, core, y):
    return lax.rem(z + lax.rem(core + y, 2) * (1 + 2 * (y // 2)), 4)


def rotation(first, count, rates):
    places = lax.broadcasted_iota(jnp.int32, (count, HD), 0) + first
    angles = places.astype(jnp.float32) * rates
    sine = jnp.sin(angles)
    lane = lax.broadcasted_iota(jnp.int32, (count, HD), 1)
    return jnp.cos(angles), jnp.where(lane < HD // 2, -sine, sine)


def blend_kernel(
    passage_ids, page_slot, offsets, recompute_blocks, rates,
    pool_k, pool_v, hidden, w_key, w_value, queries,
    out_k, out_v, part_in, stat_in,
    query_buf, slot_buf, q_group, rows_k, rows_v, outgoing, arriving_k, arriving_v, turned, fresh, fresh_in,
    hidden_buf, w_buf, t_cos, t_sin, used, send_tab, arrival_tab, send_index, arrival,
    k_buf, v_buf, acc, peak, part, stat,
    own_sem, load_sem, tp_send, tp_recv, page_send, page_recv, q_send, q_recv, f_send, f_recv,
    out_sem, kv_send, kv_recv, side_send, side_recv, part_send, part_recv,
):
    me = lax.axis_index("seq")
    my_tp = lax.axis_index("tp")
    z, y, core, half = place(me)
    barrier = pltpu.get_barrier_semaphore()

    def greet_seq(step, _):
        pl.semaphore_signal(
            barrier, inc=1, device_id={"seq": lax.rem(me + step, N_SEQ)}, device_id_type=MESH
        )
        return 0

    lax.fori_loop(1, N_SEQ, greet_seq, 0)
    for step in range(1, N_TP):
        pl.semaphore_signal(
            barrier, inc=1, device_id={"tp": lax.rem(my_tp + step, N_TP)}, device_id_type=MESH
        )

    loads = [
        pltpu.make_async_copy(hidden, hidden_buf, load_sem.at[0]),
        pltpu.make_async_copy(w_key, w_buf.at[0], load_sem.at[1]),
        pltpu.make_async_copy(w_value, w_buf.at[1], load_sem.at[2]),
        pltpu.make_async_copy(queries, query_buf, load_sem.at[5]),
        pltpu.make_async_copy(page_slot, slot_buf, load_sem.at[6]),
    ]
    for load in loads:
        load.start()

    loads[3].wait()
    my_passage = lax.rem(me, PASSAGES)
    my_start = recompute_blocks[my_passage * RB + me // PASSAGES] * BLOCK
    q_cos, q_sin = rotation(offsets[my_passage] + my_start, BLOCK, rates[...])
    for head in range(HEADS):
        cols = slice(head * HD, (head + 1) * HD)
        turned[head] = turn(query_buf[:, cols].astype(jnp.float32), q_cos, q_sin).astype(jnp.bfloat16)
    acc[...] = jnp.zeros_like(acc)
    peak[...] = jnp.full_like(peak, MASKED)
    pl.semaphore_wait(barrier, N_SEQ - 1 + N_TP - 1)

    group = lax.rem(half + core, 2)
    sibling = me + 1 - 2 * core
    bufs = (k_buf, v_buf)

    def near(step):
        return lax.rem(z + step, 4)

    def at(level):
        return level * 8 + y * 2 + core

    def keep_copy(which):
        return pltpu.make_async_copy(
            bufs[which].at[z, core], (out_k, out_v)[which], out_sem.at[which]
        )

    def kv_copy(which, step):
        return on_seq(
            bufs[which].at[z, core], bufs[which].at[z, core], kv_send.at[which, step],
            kv_recv.at[which, step], at(near(step)),
        )

    def kv_landed(which, step):
        level = near(4 - step)
        return on_seq(
            bufs[which].at[z, core], bufs[which].at[level, core], kv_send.at[which, step],
            kv_recv.at[which, step], at(level),
        )

    def side_copy(which, step):
        level = near(4 - step)
        return on_seq(
            bufs[which].at[level, core], bufs[which].at[level, core], side_send.at[which, step],
            side_recv.at[which, step], sibling,
        )

    def side_landed(which, step):
        level = near(4 - step)
        return on_seq(
            bufs[which].at[z, core], bufs[which].at[level, 1 - core], side_send.at[which, step],
            side_recv.at[which, step], sibling,
        )

    def pass_on(which):
        level, ahead = (near(3), near(1)) if which == 0 else (near(1), near(3))
        return on_seq(
            bufs[which].at[level, core], bufs[which].at[level, core], kv_send.at[which, 2],
            kv_recv.at[which, 2], at(ahead),
        )

    pools = (pool_k, pool_v)
    rows = (rows_k, rows_v)
    arriving = (arriving_k, arriving_v)

    def columns(which, owner):
        return pools[which].at[:, :, pl.ds(pl.multiple_of(owner * WIDTH, WIDTH), WIDTH)]

    def tp_copy(which, step):
        peer = lax.rem(my_tp + step, N_TP)
        return pltpu.make_async_remote_copy(
            src_ref=columns(which, peer),
            dst_ref=rows[which].at[pl.ds(my_tp * 32, 32)],
            send_sem=tp_send.at[which, step],
            recv_sem=tp_recv.at[which, step],
            device_id={"tp": peer},
            device_id_type=MESH,
        )

    def own_copy(which):
        return pltpu.make_async_copy(
            columns(which, my_tp), rows[which].at[pl.ds(my_tp * 32, 32)], own_sem.at[which]
        )

    def tp_start(which):
        for step in (1, 3, 2):
            tp_copy(which, step).start()
        own_copy(which).start()

    tp_start(0)

    group_z = group_home(z, core, y)

    def q_dest(other_y):
        return group_z * 8 + other_y * 2 + core

    def q_remote(other_y):
        return on_seq(
            turned, q_group.at[y], q_send.at[other_y], q_recv.at[y], q_dest(other_y)
        )

    def q_local():
        return pltpu.make_async_copy(turned, q_group.at[y], q_recv.at[y])

    which_block = me // PASSAGES
    home = lax.rem(me, PASSAGES) * 2

    def f_remote(side):
        return on_seq(
            fresh, fresh_in.at[which_block], f_send.at[side], f_recv.at[which_block], home + side
        )

    def f_local():
        return pltpu.make_async_copy(fresh, fresh_in.at[which_block], f_recv.at[which_block])

    far = lax.rem(y + 2, 4)

    def q_start(other_y):
        @pl.when(q_dest(other_y) != me)
        def _():
            q_remote(other_y).start()

        @pl.when(q_dest(other_y) == me)
        def _():
            q_local().start()

    for other_y in range(4):

        @pl.when(far != other_y)
        def _():
            q_start(other_y)

    tp_start(1)

    loads[4].wait()
    for row in range(PASSAGES):
        used[row : row + 1, :] = slot_buf[pl.ds(passage_ids[row], 1), :]
    slots = used[...]
    lane = lax.broadcasted_iota(jnp.int32, slots.shape, 1)
    in_half = lax.rem(lane, PER_DEST)
    hit = (slots >> 7) == me
    rank = hit.astype(jnp.int32)
    for shift in (1, 2, 4, 8, 16, 32):
        rank = rank + jnp.where(in_half >= shift, pltpu.roll(rank, shift, 1), 0)
    table = jnp.zeros(slots.shape, jnp.int32)
    for side in range(2):
        for order in range(CAP):
            wanted = hit & (rank == order + 1) & ((lane >= PER_DEST) == (side == 1))
            local = jnp.where(wanted, slots & 127, 0)
            for shift in (64, 32, 16, 8, 4, 2, 1):
                local = local + pltpu.roll(local, shift, 1)
            table = jnp.where(lane == side * CAP + order, local, table)
    send_tab[...] = table
    source = jnp.broadcast_to(used[pl.ds(me // 2, 1), :], (8, HD)) >> 7
    lane = lax.broadcasted_iota(jnp.int32, source.shape, 1)
    in_half = lax.rem(lane, PER_DEST)
    rank = jnp.zeros(source.shape, jnp.int32)
    for shift in range(1, PER_DEST):
        same = (pltpu.roll(source, shift, 1) == source) & (in_half >= shift)
        rank = rank + same.astype(jnp.int32)
    arrival_tab[...] = source * CAP + rank
    index_copies = [
        pltpu.make_async_copy(send_tab, send_index, load_sem.at[3]),
        pltpu.make_async_copy(arrival_tab, arrival, load_sem.at[4]),
    ]
    for copy in index_copies:
        copy.start()


    for load in loads[:3]:
        load.wait()

    def multiply(part, totals):
        depth = pl.ds(pl.multiple_of(part * 1024, 1024), 1024)
        return tuple(
            total
            + jnp.dot(hidden_buf[:, depth], w_buf[which, depth, :], preferred_element_type=jnp.float32)
            for which, total in enumerate(totals)
        )

    nothing = jnp.zeros((BLOCK, WIDTH), jnp.float32)
    raw_k, raw_v = lax.fori_loop(0, 8, multiply, (nothing, nothing))
    for head in range(2):
        cols = slice(head * HD, (head + 1) * HD)
        fresh[0, :, cols] = turn(raw_k[:, cols], q_cos, q_sin).astype(jnp.bfloat16)
    fresh[1] = raw_v.astype(jnp.bfloat16)
    for side in range(2):

        @pl.when(home + side != me)
        def _():
            f_remote(side).start()

        @pl.when(home + side == me)
        def _():
            f_local().start()

    token_cos, token_sin = rotation(offsets[me // 2] + core * TOK_DEV, TOK_DEV, rates[...])
    t_cos[...] = token_cos
    t_sin[...] = token_sin
    for copy in index_copies:
        copy.wait()

    def page_copy(which, step):
        peer = lax.rem(me + step, N_SEQ)
        return on_seq(
            outgoing.at[which, peer],
            arriving[which].at[me],
            page_send.at[which, step],
            page_recv.at[which, step],
            peer,
        )

    for which in range(2):
        for step in range(1, N_TP):
            peer = lax.rem(my_tp + N_TP - step, N_TP)
            pltpu.make_async_remote_copy(
                src_ref=columns(which, my_tp),
                dst_ref=rows[which].at[pl.ds(peer * 32, 32)],
                send_sem=tp_send.at[which, step],
                recv_sem=tp_recv.at[which, step],
                device_id={"tp": peer},
                device_id_type=MESH,
            ).wait_recv()
        own_copy(which).wait()

        def pick(step):
            peer = lax.rem(me + step, N_SEQ)
            for rank in range(CAP):
                outgoing[which, peer, rank] = rows[which][
                    send_index[peer // 2, lax.rem(peer, 2) * CAP + rank]
                ]

        def pick_and_send(part, _):
            for number in range(5):
                step = part * 5 + number + 1
                pick(step)
                page_copy(which, step).start()
            return 0

        lax.fori_loop(0, 6, pick_and_send, 0)
        pick(31)
        page_copy(which, 31).start()
        pick(0)
        arriving[which][me] = outgoing[which, me]

    q_start(far)

    def q_landed(slot):
        return on_seq(turned, q_group.at[slot], q_send.at[0], q_recv.at[slot], me)

    for slot in range(4):

        @pl.when(far != slot)
        def _():
            q_landed(slot).wait_recv()

    for slot in range(2):
        on_seq(fresh, fresh_in.at[slot], f_send.at[0], f_recv.at[slot], me).wait_recv()

    for which in range(2):

        def landed(step, _):
            sender = lax.rem(me + N_SEQ - step, N_SEQ)
            on_seq(
                outgoing.at[which, me],
                arriving[which].at[sender],
                page_send.at[which, step],
                page_recv.at[which, step],
                sender,
            ).wait_recv()
            return 0

        lax.fori_loop(1, N_SEQ, landed, 0)

        def put(index, _):
            block = core * 8 + index
            first, second = (recompute_blocks[me // 2 * RB + number] for number in range(RB))
            here = jnp.full((PAGE, WIDTH), block, jnp.int32)
            flag = (here == first) | (here == second)
            for page in range(8):
                slot = arrival[0, core * PER_DEST + index * 8 + page]
                where = pl.ds(pl.multiple_of(index * BLOCK + page * PAGE, PAGE), PAGE)
                got = arriving[which][slot // CAP, lax.rem(slot, CAP)].astype(jnp.float32)
                if which == 0:
                    cosine, sine = t_cos[where], t_sin[where]
                    got = jnp.concatenate(
                        [turn(got[:, :HD], cosine, sine), turn(got[:, HD:], cosine, sine)], axis=1
                    )
                within = slice(page * PAGE, (page + 1) * PAGE)
                new = fresh_in[jnp.where(second == block, 1, 0), which, within]
                mixed = jnp.where(flag, new.astype(jnp.float32), got)
                bufs[which][z, core, where] = mixed.astype(jnp.bfloat16)
            return 0

        lax.fori_loop(0, 8, put, 0)
        keep_copy(which).start()
        side_copy(which, 0).start()
        for step in (1, 3):
            kv_copy(which, step).start()

    ones = jnp.ones((PASSAGE_LEN, HD), jnp.bfloat16)

    def fold(slot, level, limit):
        if limit is not None:
            shape = (QT, PASSAGE_LEN)
            ahead = lax.broadcasted_iota(jnp.int32, shape, 1) - (
                lax.broadcasted_iota(jnp.int32, shape, 0) & (BLOCK - 1)
            )
        for index in range(8 // UNIT):
            for kv in range(2):
                cols = slice(kv * HD, (kv + 1) * HD)
                heads = slice(kv * 8 + index * UNIT, kv * 8 + (index + 1) * UNIT)
                q = q_group[slot, heads].reshape(QT, HD)
                keys = k_buf[level].reshape(PASSAGE_LEN, WIDTH)[:, cols]
                values = v_buf[level].reshape(PASSAGE_LEN, WIDTH)[:, cols]
                score = lax.dot_general(q, keys, BY_KEY, preferred_element_type=jnp.float32)
                if limit is not None:
                    score = jnp.where(ahead <= limit, score, MASKED)
                old = peak[slot, heads].reshape(QT, HD)
                new = jnp.maximum(old, jnp.max(score, axis=1, keepdims=True))
                keep = jnp.exp2((old - new) * EXPONENT)
                weight = jnp.exp2((score - new[:, :1]) * EXPONENT).astype(jnp.bfloat16)
                total = jnp.dot(
                    weight,
                    jnp.concatenate([values, ones], axis=1),
                    preferred_element_type=jnp.float32,
                )
                before = acc[slot, heads].reshape(QT, 2 * HD)
                acc[slot, heads] = (before * keep[:, :1] + total).reshape(UNIT, BLOCK, 2 * HD)
                peak[slot, heads] = new.reshape(UNIT, BLOCK, HD)

    def slot_passage(slot):
        return lax.rem(group + slot, 2) * 8 + 2 * slot + core

    def visit(slot, level):
        passage = level * 4 + y
        mine = slot_passage(slot)

        @pl.when(passage < mine)
        def _():
            fold(slot, level, None)

        @pl.when(passage == mine)
        def _():
            fold(slot, level, recompute_blocks[mine * RB + home_level(z, core, slot) // 2] * BLOCK)

    def owner(slot):
        return home_level(z, core, slot) * 8 + slot * 2 + core

    def part_copies(slot):
        return (
            on_seq(part.at[slot], part_in.at[y], part_send.at[0, slot], part_recv.at[0, y],
                   owner(slot)),
            on_seq(stat.at[slot], stat_in.at[y], part_send.at[1, slot], part_recv.at[1, y],
                   owner(slot)),
        )

    def local_copies(slot):
        return (
            pltpu.make_async_copy(part.at[slot], part_in.at[y], part_recv.at[0, y]),
            pltpu.make_async_copy(stat.at[slot], stat_in.at[y], part_recv.at[1, y]),
        )

    def give_back(slot):
        lane = lax.broadcasted_iota(jnp.int32, (BLOCK, HD), 1)

        def head_part(head, logs):
            total = acc[slot, head]
            weight_sum = total[:, HD:]
            some = weight_sum > 0.0
            safe = jnp.where(some, weight_sum, 1.0)
            part[slot, head] = (total[:, :HD] / safe).astype(jnp.bfloat16)
            size = jnp.where(some, peak[slot, head] * EXPONENT + jnp.log2(safe), MASKED)
            return jnp.where(lane == head, size, logs)

        stat[slot] = lax.fori_loop(
            0, HEADS, head_part, jnp.full((BLOCK, HD), MASKED, jnp.float32), unroll=4
        )

        @pl.when(owner(slot) != me)
        def _():
            for copy in part_copies(slot):
                copy.start()

        @pl.when(owner(slot) == me)
        def _():
            for copy in local_copies(slot):
                copy.start()

    def ranked(order):
        return 2 * lax.rem(order, 2) + lax.rem(order // 2 + group, 2)

    far_order = sum(jnp.where(ranked(3 - order) == far, order, 0) for order in range(4))
    soon = jnp.where((z == 1) | (z == 2), 1, 3)
    later = 4 - soon

    def sees(slot, level):
        return slot_passage(slot) >= level * 4 + y

    def unfinished(slot):
        return sees(slot, near(4 - later)) | sees(slot, near(2))

    def arrive(turn_index, _):
        @pl.when(turn_index == 0)
        def _():
            for which in range(2):
                side_landed(which, 0).wait_recv()

        @pl.when(turn_index == 1)
        def _():
            kv_landed(1, 1).wait_recv()
            side_copy(1, 1).start()
            kv_landed(0, 3).wait_recv()
            side_copy(0, 3).start()
            for which in range(2):
                side_landed(which, soon).wait_recv()

        @pl.when(turn_index == 2)
        def _():
            def early(order, _):
                slot = ranked(order)

                @pl.when(jnp.logical_not(unfinished(slot)))
                def _():
                    give_back(slot)

                return 0

            lax.fori_loop(0, 4, early, 0)
            for which in range(2):
                kv_landed(which, 2).wait_recv()
                side_copy(which, 2).start()
                side_landed(which, later).wait_recv()
            for which in range(2):
                side_landed(which, 2).wait_recv()

        def each(order, _):
            skip = jnp.where((turn_index == 0) & (order >= far_order), 1, 0)
            picked = ranked(jnp.where(turn_index == 2, order // 2, 3 - lax.rem(order + skip, 4)))
            last = (turn_index == 0) & (order == 3)
            slot = jnp.where(last, far, picked)
            step = jnp.where(
                turn_index == 2,
                jnp.where(lax.rem(order, 2) == 0, later, 2),
                jnp.where(turn_index == 1, soon, 0),
            )

            @pl.when(last)
            def _():
                q_landed(far).wait_recv()

            visit(slot, near(4 - step))

            @pl.when((turn_index == 0) & (order == 1))
            def _():
                kv_landed(0, 1).wait_recv()
                pass_on(0).start()
                side_copy(0, 1).start()

            @pl.when((turn_index == 0) & (order == 3))
            def _():
                kv_landed(1, 3).wait_recv()
                pass_on(1).start()
                side_copy(1, 3).start()

            @pl.when((turn_index == 2) & (lax.rem(order, 2) == 1) & unfinished(slot))
            def _():
                give_back(slot)

            return 0

        lax.fori_loop(0, jnp.where(turn_index == 2, 8, 4), each, 0)
        return 0

    lax.fori_loop(0, 3, arrive, 0)

    for slot in range(4):
        on_seq(part.at[0], part_in.at[slot], part_send.at[0, 0], part_recv.at[0, slot],
               me).wait_recv()
        on_seq(stat.at[0], stat_in.at[slot], part_send.at[1, 0], part_recv.at[1, slot],
               me).wait_recv()
    for which in range(2):
        for step in (1, 3):
            kv_copy(which, step).wait_send()
        pass_on(which).wait_send()
        for step in range(4):
            side_copy(which, step).wait_send()
    for slot in range(4):

        @pl.when(owner(slot) != me)
        def _():
            for copy in part_copies(slot):
                copy.wait_send()
    for which in range(2):
        keep_copy(which).wait()
    for which in range(2):
        for step in range(1, N_TP):
            tp_copy(which, step).wait_send()

        def sent(step, _):
            page_copy(which, step).wait_send()
            return 0

        lax.fori_loop(1, N_SEQ, sent, 0)
    for other_y in range(4):

        @pl.when(q_dest(other_y) != me)
        def _():
            q_remote(other_y).wait_send()

    for side in range(2):

        @pl.when(home + side != me)
        def _():
            f_remote(side).wait_send()


def merge_kernel(key_in, value_in, parts, stats, key_out, value_out, attended):
    key_out[...] = key_in[...]
    value_out[...] = value_in[...]
    logs = [stats[slot] for slot in range(4)]
    top = jnp.maximum(jnp.maximum(logs[0], logs[1]), jnp.maximum(logs[2], logs[3]))
    shares = [jnp.exp2(log - top) for log in logs]
    whole = 1.0 / (shares[0] + shares[1] + shares[2] + shares[3])
    shares = [share * whole for share in shares]
    lane = lax.broadcasted_iota(jnp.int32, (BLOCK, HD), 1)
    for index in range(HEADS // 2):
        mine = lane == pl.program_id(0) * (HEADS // 2) + index
        result = sum(
            parts[slot, index].astype(jnp.float32)
            * jnp.sum(jnp.where(mine, shares[slot], 0.0), axis=1, keepdims=True)
            for slot in range(4)
        )
        attended[:, index * HD : (index + 1) * HD] = result.astype(jnp.bfloat16)


def on_device(
    pool_keys,
    pool_values,
    passage_ids,
    page_slot,
    offsets,
    recompute_blocks,
    hidden_rows,
    w_key,
    w_value,
    queries,
):
    rates = jnp.asarray(frequencies())
    vmem = pl.BlockSpec(memory_space=pltpu.VMEM)
    smem = pl.BlockSpec(memory_space=pltpu.SMEM)
    hbm = pl.BlockSpec(memory_space=pltpu.HBM)
    bf16 = jnp.bfloat16
    dma = pltpu.SemaphoreType.DMA
    cache = jax.ShapeDtypeStruct((TOK_DEV, WIDTH), bf16)
    made = pl.pallas_call(
        blend_kernel,
        out_shape=[
            cache,
            cache,
            jax.ShapeDtypeStruct((4, HEADS, BLOCK, HD), bf16),
            jax.ShapeDtypeStruct((4, BLOCK, HD), jnp.float32),
        ],
        in_specs=[smem, hbm, smem, smem, vmem, hbm, hbm, hbm, hbm, hbm, hbm],
        out_specs=[hbm, hbm, hbm, hbm],
        scratch_shapes=[
            pltpu.VMEM((BLOCK, HEADS * HD), bf16),
            pltpu.VMEM((32, HD), jnp.int32),
            pltpu.VMEM((4, HEADS, BLOCK, HD), bf16),
            pltpu.VMEM((128, PAGE, WIDTH), bf16),
            pltpu.VMEM((128, PAGE, WIDTH), bf16),
            pltpu.VMEM((2, N_SEQ, CAP, PAGE, WIDTH), bf16),
            pltpu.VMEM((N_SEQ, CAP, PAGE, WIDTH), bf16),
            pltpu.VMEM((N_SEQ, CAP, PAGE, WIDTH), bf16),
            pltpu.VMEM((HEADS, BLOCK, HD), bf16),
            pltpu.VMEM((2, BLOCK, WIDTH), bf16),
            pltpu.VMEM((RB, 2, BLOCK, WIDTH), bf16),
            pltpu.VMEM((BLOCK, 8192), bf16),
            pltpu.VMEM((2, 8192, WIDTH), bf16),
            pltpu.VMEM((TOK_DEV, HD), jnp.float32),
            pltpu.VMEM((TOK_DEV, HD), jnp.float32),
            pltpu.VMEM((PASSAGES, HD), jnp.int32),
            pltpu.VMEM((PASSAGES, HD), jnp.int32),
            pltpu.VMEM((8, HD), jnp.int32),
            pltpu.SMEM((PASSAGES, HD), jnp.int32),
            pltpu.SMEM((8, HD), jnp.int32),
            pltpu.VMEM((4, 2, TOK_DEV, WIDTH), bf16),
            pltpu.VMEM((4, 2, TOK_DEV, WIDTH), bf16),
            pltpu.VMEM((4, HEADS, BLOCK, 2 * HD), jnp.float32),
            pltpu.VMEM((4, HEADS, BLOCK, HD), jnp.float32),
            pltpu.VMEM((4, HEADS, BLOCK, HD), bf16),
            pltpu.VMEM((4, BLOCK, HD), jnp.float32),
            dma((2,)),
            dma((7,)),
            dma((2, N_TP)),
            dma((2, N_TP)),
            dma((2, N_SEQ)),
            dma((2, N_SEQ)),
            dma((4,)),
            dma((4,)),
            dma((2,)),
            dma((2,)),
            dma((2,)),
            dma((2, 4)),
            dma((2, 4)),
            dma((2, 4)),
            dma((2, 4)),
            dma((2, 4)),
            dma((2, 4)),
        ],
        compiler_params=pltpu.CompilerParams(
            collective_id=0, has_side_effects=True, vmem_limit_bytes=60 * 2**20
        ),
        name="blend_and_attend",
    )(
        passage_ids, page_slot, offsets, recompute_blocks.reshape(-1), rates,
        pool_keys, pool_values, hidden_rows, w_key, w_value, queries,
    )
    slab = pl.BlockSpec((TOK_DEV // 2, WIDTH), lambda i: (i, 0))
    return tuple(
        pl.pallas_call(
            merge_kernel,
            out_shape=[cache, cache, jax.ShapeDtypeStruct((BLOCK, HEADS * HD), bf16)],
            grid=(2,),
            in_specs=[
                slab,
                slab,
                pl.BlockSpec((4, HEADS // 2, BLOCK, HD), lambda i: (0, i, 0, 0)),
                pl.BlockSpec((4, BLOCK, HD), lambda i: (0, 0, 0)),
            ],
            out_specs=[slab, slab, pl.BlockSpec((BLOCK, HEADS * HD // 2), lambda i: (0, i))],
            name="merge",
        )(*made)
    )


def solution(mesh):
    placed = (
        P(("seq", "tp"), None, None),
        P(("seq", "tp"), None, None),
        P(),
        P(),
        P(),
        P(),
        P("seq", None),
        P(None, "tp"),
        P(None, "tp"),
        P("seq", "tp"),
    )
    return jax.shard_map(
        on_device,
        mesh=mesh,
        in_specs=placed,
        out_specs=(P("seq", "tp"), P("seq", "tp"), P("seq", "tp")),
        check_vma=False,
    )
```

```python
import math

import jax
import jax.numpy as jnp
import numpy as np
from jax import lax
from jax.experimental import pallas as pl
from jax.experimental.pallas import tpu as pltpu
from jax.sharding import PartitionSpec as P

HD = 128
PASSAGE_LEN = 2048
BLOCK = 128
PAGE = 16
RB = 2
TOK_DEV = 1024
CAP = 4
N_SEQ = 32
N_TP = 4
PASSAGES = 16
PER_DEST = TOK_DEV // PAGE
WIDTH = 256
HEADS = 16
MASKED = -1e30
EXPONENT = math.log2(math.e) / math.sqrt(HD)
QT = 256
UNIT = QT // BLOCK
BY_KEY = (((1,), (1,)), ((), ()))
MESH = pl.DeviceIdType.MESH


def frequencies():
    base_rate = 500000.0 ** (-np.arange(0, HD, 2) / HD)
    wave_length = 2.0 * math.pi / base_rate
    smooth = (8192.0 / wave_length - 1.0) / 3.0
    blended = (1.0 - smooth) * base_rate / 8.0 + smooth * base_rate
    rates = np.where(
        wave_length > 8192.0, base_rate / 8.0, np.where(wave_length < 2048.0, base_rate, blended)
    )
    return np.concatenate([rates, rates])[None, :].astype(np.float32)


def turn(values, cosine, sine):
    return values * cosine + pltpu.roll(values, HD // 2, 1) * sine


def on_seq(source, target, send_sem, recv_sem, peer):
    return pltpu.make_async_remote_copy(
        src_ref=source,
        dst_ref=target,
        send_sem=send_sem,
        recv_sem=recv_sem,
        device_id={"seq": peer},
        device_id_type=MESH,
    )


def place(me):
    z = me // 8
    return z, (me // 2) % 4, me % 2, z % 2


def home_level(z, core, slot):
    return lax.rem(z + lax.rem(core + slot, 2) * (3 - 2 * (slot // 2)), 4)


def group_home(z, core, y):
    return lax.rem(z + lax.rem(core + y, 2) * (1 + 2 * (y // 2)), 4)


def rotation(first, count, rates):
    places = lax.broadcasted_iota(jnp.int32, (count, HD), 0) + first
    angles = places.astype(jnp.float32) * rates
    sine = jnp.sin(angles)
    lane = lax.broadcasted_iota(jnp.int32, (count, HD), 1)
    return jnp.cos(angles), jnp.where(lane < HD // 2, -sine, sine)


def blend_kernel(
    passage_ids, page_slot, offsets, recompute_blocks, rates,
    pool_k, pool_v, hidden, w_key, w_value, queries,
    out_k, out_v, part_in, stat_in,
    query_buf, slot_buf, q_group, rows_k, rows_v, outgoing, arriving_k, arriving_v, turned, fresh, fresh_in,
    hidden_buf, w_buf, t_cos, t_sin, used, send_tab, arrival_tab, send_index, arrival,
    k_buf, v_buf, acc, peak, part, stat,
    own_sem, load_sem, tp_send, tp_recv, page_send, page_recv, q_send, q_recv, f_send, f_recv,
    out_sem, kv_send, kv_recv, side_send, side_recv, part_send, part_recv,
):
    me = lax.axis_index("seq")
    my_tp = lax.axis_index("tp")
    z, y, core, half = place(me)
    barrier = pltpu.get_barrier_semaphore()

    def greet_seq(step, _):
        pl.semaphore_signal(
            barrier, inc=1, device_id={"seq": lax.rem(me + step, N_SEQ)}, device_id_type=MESH
        )
        return 0

    lax.fori_loop(1, N_SEQ, greet_seq, 0)
    for step in range(1, N_TP):
        pl.semaphore_signal(
            barrier, inc=1, device_id={"tp": lax.rem(my_tp + step, N_TP)}, device_id_type=MESH
        )

    loads = [
        pltpu.make_async_copy(hidden, hidden_buf, load_sem.at[0]),
        pltpu.make_async_copy(w_key, w_buf.at[0], load_sem.at[1]),
        pltpu.make_async_copy(w_value, w_buf.at[1], load_sem.at[2]),
        pltpu.make_async_copy(queries, query_buf, load_sem.at[5]),
        pltpu.make_async_copy(page_slot, slot_buf, load_sem.at[6]),
    ]
    for load in loads:
        load.start()

    loads[3].wait()
    my_passage = lax.rem(me, PASSAGES)
    my_start = recompute_blocks[me // PASSAGES, my_passage] * BLOCK
    q_cos, q_sin = rotation(offsets[my_passage] + my_start, BLOCK, rates[...])
    for head in range(HEADS):
        cols = slice(head * HD, (head + 1) * HD)
        turned[head] = turn(query_buf[:, cols].astype(jnp.float32), q_cos, q_sin).astype(jnp.bfloat16)
    acc[...] = jnp.zeros_like(acc)
    peak[...] = jnp.full_like(peak, MASKED)
    pl.semaphore_wait(barrier, N_SEQ - 1 + N_TP - 1)

    group = lax.rem(half + core, 2)
    sibling = me + 1 - 2 * core
    bufs = (k_buf, v_buf)

    def near(step):
        return lax.rem(z + step, 4)

    def at(level):
        return level * 8 + y * 2 + core

    def keep_copy(which):
        return pltpu.make_async_copy(
            bufs[which].at[z, core], (out_k, out_v)[which], out_sem.at[which]
        )

    def kv_copy(which, step):
        return on_seq(
            bufs[which].at[z, core], bufs[which].at[z, core], kv_send.at[which, step],
            kv_recv.at[which, step], at(near(step)),
        )

    def kv_landed(which, step):
        level = near(4 - step)
        return on_seq(
            bufs[which].at[z, core], bufs[which].at[level, core], kv_send.at[which, step],
            kv_recv.at[which, step], at(level),
        )

    def side_copy(which, step):
        level = near(4 - step)
        return on_seq(
            bufs[which].at[level, core], bufs[which].at[level, core], side_send.at[which, step],
            side_recv.at[which, step], sibling,
        )

    def side_landed(which, step):
        level = near(4 - step)
        return on_seq(
            bufs[which].at[z, core], bufs[which].at[level, 1 - core], side_send.at[which, step],
            side_recv.at[which, step], sibling,
        )

    def pass_on(which):
        level, ahead = (near(3), near(1)) if which == 0 else (near(1), near(3))
        return on_seq(
            bufs[which].at[level, core], bufs[which].at[level, core], kv_send.at[which, 2],
            kv_recv.at[which, 2], at(ahead),
        )

    pools = (pool_k, pool_v)
    rows = (rows_k, rows_v)
    arriving = (arriving_k, arriving_v)

    def columns(which, owner):
        return pools[which].at[:, :, pl.ds(pl.multiple_of(owner * WIDTH, WIDTH), WIDTH)]

    def tp_copy(which, step):
        peer = lax.rem(my_tp + step, N_TP)
        return pltpu.make_async_remote_copy(
            src_ref=columns(which, peer),
            dst_ref=rows[which].at[pl.ds(my_tp * 32, 32)],
            send_sem=tp_send.at[which, step],
            recv_sem=tp_recv.at[which, step],
            device_id={"tp": peer},
            device_id_type=MESH,
        )

    def own_copy(which):
        return pltpu.make_async_copy(
            columns(which, my_tp), rows[which].at[pl.ds(my_tp * 32, 32)], own_sem.at[which]
        )

    def tp_start(which):
        for step in (1, 3, 2):
            tp_copy(which, step).start()
        own_copy(which).start()

    tp_start(0)

    group_z = group_home(z, core, y)

    def q_dest(other_y):
        return group_z * 8 + other_y * 2 + core

    def q_remote(other_y):
        return on_seq(
            turned, q_group.at[y], q_send.at[other_y], q_recv.at[y], q_dest(other_y)
        )

    def q_local():
        return pltpu.make_async_copy(turned, q_group.at[y], q_recv.at[y])

    which_block = me // PASSAGES
    home = lax.rem(me, PASSAGES) * 2

    def f_remote(side):
        return on_seq(
            fresh, fresh_in.at[which_block], f_send.at[side], f_recv.at[which_block], home + side
        )

    def f_local():
        return pltpu.make_async_copy(fresh, fresh_in.at[which_block], f_recv.at[which_block])

    far = lax.rem(y + 2, 4)

    def q_start(other_y):
        @pl.when(q_dest(other_y) != me)
        def _():
            q_remote(other_y).start()

        @pl.when(q_dest(other_y) == me)
        def _():
            q_local().start()

    for other_y in range(4):

        @pl.when(far != other_y)
        def _():
            q_start(other_y)

    tp_start(1)

    loads[4].wait()
    for row in range(PASSAGES):
        used[row : row + 1, :] = slot_buf[pl.ds(passage_ids[row], 1), :]
    slots = used[...]
    lane = lax.broadcasted_iota(jnp.int32, slots.shape, 1)
    in_half = lax.rem(lane, PER_DEST)
    hit = (slots >> 7) == me
    rank = hit.astype(jnp.int32)
    for shift in (1, 2, 4, 8, 16, 32):
        rank = rank + jnp.where(in_half >= shift, pltpu.roll(rank, shift, 1), 0)
    table = jnp.zeros(slots.shape, jnp.int32)
    for side in range(2):
        for order in range(CAP):
            wanted = hit & (rank == order + 1) & ((lane >= PER_DEST) == (side == 1))
            local = jnp.where(wanted, slots & 127, 0)
            for shift in (64, 32, 16, 8, 4, 2, 1):
                local = local + pltpu.roll(local, shift, 1)
            table = jnp.where(lane == side * CAP + order, local, table)
    send_tab[...] = table
    source = jnp.broadcast_to(used[pl.ds(me // 2, 1), :], (8, HD)) >> 7
    lane = lax.broadcasted_iota(jnp.int32, source.shape, 1)
    in_half = lax.rem(lane, PER_DEST)
    rank = jnp.zeros(source.shape, jnp.int32)
    for shift in range(1, PER_DEST):
        same = (pltpu.roll(source, shift, 1) == source) & (in_half >= shift)
        rank = rank + same.astype(jnp.int32)
    arrival_tab[...] = source * CAP + rank
    index_copies = [
        pltpu.make_async_copy(send_tab, send_index, load_sem.at[3]),
        pltpu.make_async_copy(arrival_tab, arrival, load_sem.at[4]),
    ]
    for copy in index_copies:
        copy.start()


    for load in loads[:3]:
        load.wait()

    def multiply(part, totals):
        depth = pl.ds(pl.multiple_of(part * 1024, 1024), 1024)
        return tuple(
            total
            + jnp.dot(hidden_buf[:, depth], w_buf[which, depth, :], preferred_element_type=jnp.float32)
            for which, total in enumerate(totals)
        )

    nothing = jnp.zeros((BLOCK, WIDTH), jnp.float32)
    raw_k, raw_v = lax.fori_loop(0, 8, multiply, (nothing, nothing))
    for head in range(2):
        cols = slice(head * HD, (head + 1) * HD)
        fresh[0, :, cols] = turn(raw_k[:, cols], q_cos, q_sin).astype(jnp.bfloat16)
    fresh[1] = raw_v.astype(jnp.bfloat16)
    for side in range(2):

        @pl.when(home + side != me)
        def _():
            f_remote(side).start()

        @pl.when(home + side == me)
        def _():
            f_local().start()

    token_cos, token_sin = rotation(offsets[me // 2] + core * TOK_DEV, TOK_DEV, rates[...])
    t_cos[...] = token_cos
    t_sin[...] = token_sin
    for copy in index_copies:
        copy.wait()

    def page_copy(which, step):
        peer = lax.rem(me + step, N_SEQ)
        return on_seq(
            outgoing.at[which, peer],
            arriving[which].at[me],
            page_send.at[which, step],
            page_recv.at[which, step],
            peer,
        )

    for which in range(2):
        for step in range(1, N_TP):
            peer = lax.rem(my_tp + N_TP - step, N_TP)
            pltpu.make_async_remote_copy(
                src_ref=columns(which, my_tp),
                dst_ref=rows[which].at[pl.ds(peer * 32, 32)],
                send_sem=tp_send.at[which, step],
                recv_sem=tp_recv.at[which, step],
                device_id={"tp": peer},
                device_id_type=MESH,
            ).wait_recv()
        own_copy(which).wait()

        def pick(step):
            peer = lax.rem(me + step, N_SEQ)
            for rank in range(CAP):
                outgoing[which, peer, rank] = rows[which][
                    send_index[peer // 2, lax.rem(peer, 2) * CAP + rank]
                ]

        def pick_and_send(part, _):
            for number in range(5):
                step = part * 5 + number + 1
                pick(step)
                page_copy(which, step).start()
            return 0

        lax.fori_loop(0, 6, pick_and_send, 0)
        pick(31)
        page_copy(which, 31).start()
        pick(0)
        arriving[which][me] = outgoing[which, me]

    q_start(far)

    def q_landed(slot):
        return on_seq(turned, q_group.at[slot], q_send.at[0], q_recv.at[slot], me)

    for slot in range(4):

        @pl.when(far != slot)
        def _():
            q_landed(slot).wait_recv()

    for slot in range(2):
        on_seq(fresh, fresh_in.at[slot], f_send.at[0], f_recv.at[slot], me).wait_recv()

    for which in range(2):

        def landed(step, _):
            sender = lax.rem(me + N_SEQ - step, N_SEQ)
            on_seq(
                outgoing.at[which, me],
                arriving[which].at[sender],
                page_send.at[which, step],
                page_recv.at[which, step],
                sender,
            ).wait_recv()
            return 0

        lax.fori_loop(1, N_SEQ, landed, 0)

        def put(index, _):
            block = core * 8 + index
            first, second = (recompute_blocks[number, me // 2] for number in range(RB))
            here = jnp.full((PAGE, WIDTH), block, jnp.int32)
            flag = (here == first) | (here == second)
            for page in range(8):
                slot = arrival[0, core * PER_DEST + index * 8 + page]
                where = pl.ds(pl.multiple_of(index * BLOCK + page * PAGE, PAGE), PAGE)
                got = arriving[which][slot // CAP, lax.rem(slot, CAP)].astype(jnp.float32)
                if which == 0:
                    cosine, sine = t_cos[where], t_sin[where]
                    got = jnp.concatenate(
                        [turn(got[:, :HD], cosine, sine), turn(got[:, HD:], cosine, sine)], axis=1
                    )
                within = slice(page * PAGE, (page + 1) * PAGE)
                new = fresh_in[jnp.where(second == block, 1, 0), which, within]
                mixed = jnp.where(flag, new.astype(jnp.float32), got)
                bufs[which][z, core, where] = mixed.astype(jnp.bfloat16)
            return 0

        lax.fori_loop(0, 8, put, 0)
        keep_copy(which).start()
        side_copy(which, 0).start()
        for step in (1, 3):
            kv_copy(which, step).start()

    ones = jnp.ones((PASSAGE_LEN, HD), jnp.bfloat16)

    def fold(slot, level, limit):
        if limit is not None:
            shape = (QT, PASSAGE_LEN)
            ahead = lax.broadcasted_iota(jnp.int32, shape, 1) - (
                lax.broadcasted_iota(jnp.int32, shape, 0) & (BLOCK - 1)
            )
        for index in range(8 // UNIT):
            for kv in range(2):
                cols = slice(kv * HD, (kv + 1) * HD)
                heads = slice(kv * 8 + index * UNIT, kv * 8 + (index + 1) * UNIT)
                q = q_group[slot, heads].reshape(QT, HD)
                keys = k_buf[level].reshape(PASSAGE_LEN, WIDTH)[:, cols]
                values = v_buf[level].reshape(PASSAGE_LEN, WIDTH)[:, cols]
                score = lax.dot_general(q, keys, BY_KEY, preferred_element_type=jnp.float32)
                if limit is not None:
                    score = jnp.where(ahead <= limit, score, MASKED)
                old = peak[slot, heads].reshape(QT, HD)
                new = jnp.maximum(old, jnp.max(score, axis=1, keepdims=True))
                keep = jnp.exp2((old - new) * EXPONENT)
                weight = jnp.exp2((score - new[:, :1]) * EXPONENT).astype(jnp.bfloat16)
                total = jnp.dot(
                    weight,
                    jnp.concatenate([values, ones], axis=1),
                    preferred_element_type=jnp.float32,
                )
                before = acc[slot, heads].reshape(QT, 2 * HD)
                acc[slot, heads] = (before * keep[:, :1] + total).reshape(UNIT, BLOCK, 2 * HD)
                peak[slot, heads] = new.reshape(UNIT, BLOCK, HD)

    def slot_passage(slot):
        return lax.rem(group + slot, 2) * 8 + 2 * slot + core

    def visit(slot, level):
        passage = level * 4 + y
        mine = slot_passage(slot)

        @pl.when(passage < mine)
        def _():
            fold(slot, level, None)

        @pl.when(passage == mine)
        def _():
            fold(slot, level, recompute_blocks[home_level(z, core, slot) // 2, mine] * BLOCK)

    def owner(slot):
        return home_level(z, core, slot) * 8 + slot * 2 + core

    def part_copies(slot):
        return (
            on_seq(part.at[slot], part_in.at[y], part_send.at[0, slot], part_recv.at[0, y],
                   owner(slot)),
            on_seq(stat.at[slot], stat_in.at[y], part_send.at[1, slot], part_recv.at[1, y],
                   owner(slot)),
        )

    def local_copies(slot):
        return (
            pltpu.make_async_copy(part.at[slot], part_in.at[y], part_recv.at[0, y]),
            pltpu.make_async_copy(stat.at[slot], stat_in.at[y], part_recv.at[1, y]),
        )

    def give_back(slot):
        lane = lax.broadcasted_iota(jnp.int32, (BLOCK, HD), 1)

        def head_part(head, logs):
            total = acc[slot, head]
            weight_sum = total[:, HD:]
            some = weight_sum > 0.0
            safe = jnp.where(some, weight_sum, 1.0)
            part[slot, head] = (total[:, :HD] / safe).astype(jnp.bfloat16)
            size = jnp.where(some, peak[slot, head] * EXPONENT + jnp.log2(safe), MASKED)
            return jnp.where(lane == head, size, logs)

        stat[slot] = lax.fori_loop(
            0, HEADS, head_part, jnp.full((BLOCK, HD), MASKED, jnp.float32), unroll=4
        )

        @pl.when(owner(slot) != me)
        def _():
            for copy in part_copies(slot):
                copy.start()

        @pl.when(owner(slot) == me)
        def _():
            for copy in local_copies(slot):
                copy.start()

    def ranked(order):
        return 2 * lax.rem(order, 2) + lax.rem(order // 2 + group, 2)

    far_order = sum(jnp.where(ranked(3 - order) == far, order, 0) for order in range(4))
    soon = jnp.where((z == 1) | (z == 2), 1, 3)
    later = 4 - soon

    def sees(slot, level):
        return slot_passage(slot) >= level * 4 + y

    def unfinished(slot):
        return sees(slot, near(4 - later)) | sees(slot, near(2))

    def hand_over(step):
        @pl.when(step == 1)
        def _():
            kv_landed(1, 1).wait_recv()
            side_copy(1, 1).start()

        @pl.when(step == 3)
        def _():
            kv_landed(0, 3).wait_recv()
            side_copy(0, 3).start()

    def arrive(turn_index, _):
        @pl.when(turn_index == 0)
        def _():
            for which in range(2):
                side_landed(which, 0).wait_recv()

        @pl.when(turn_index == 1)
        def _():
            hand_over(soon)
            for which in range(2):
                side_landed(which, soon).wait_recv()

        @pl.when(turn_index == 2)
        def _():
            def early(order, _):
                slot = ranked(order)

                @pl.when(jnp.logical_not(unfinished(slot)))
                def _():
                    give_back(slot)

                return 0

            lax.fori_loop(0, 4, early, 0)
            for which in range(2):
                kv_landed(which, 2).wait_recv()
                side_copy(which, 2).start()
                side_landed(which, later).wait_recv()
            for which in range(2):
                side_landed(which, 2).wait_recv()

        def each(order, _):
            skip = jnp.where((turn_index == 0) & (order >= far_order), 1, 0)
            picked = ranked(jnp.where(turn_index == 2, order // 2, 3 - lax.rem(order + skip, 4)))
            last = (turn_index == 0) & (order == 3)
            slot = jnp.where(last, far, picked)
            step = jnp.where(
                turn_index == 2,
                jnp.where(lax.rem(order, 2) == 0, later, 2),
                jnp.where(turn_index == 1, soon, 0),
            )

            @pl.when(last)
            def _():
                q_landed(far).wait_recv()

            visit(slot, near(4 - step))

            @pl.when((turn_index == 1) & (order == 1))
            def _():
                hand_over(later)

            @pl.when((turn_index == 0) & (order == 1))
            def _():
                kv_landed(0, 1).wait_recv()
                pass_on(0).start()
                side_copy(0, 1).start()

            @pl.when((turn_index == 0) & (order == 3))
            def _():
                kv_landed(1, 3).wait_recv()
                pass_on(1).start()
                side_copy(1, 3).start()

            @pl.when((turn_index == 2) & (lax.rem(order, 2) == 1) & unfinished(slot))
            def _():
                give_back(slot)

            return 0

        lax.fori_loop(0, jnp.where(turn_index == 2, 8, 4), each, 0)
        return 0

    lax.fori_loop(0, 3, arrive, 0)

    for slot in range(4):
        on_seq(part.at[0], part_in.at[slot], part_send.at[0, 0], part_recv.at[0, slot],
               me).wait_recv()
        on_seq(stat.at[0], stat_in.at[slot], part_send.at[1, 0], part_recv.at[1, slot],
               me).wait_recv()
    for which in range(2):
        for step in (1, 3):
            kv_copy(which, step).wait_send()
        pass_on(which).wait_send()
        for step in range(4):
            side_copy(which, step).wait_send()
    for slot in range(4):

        @pl.when(owner(slot) != me)
        def _():
            for copy in part_copies(slot):
                copy.wait_send()
    for which in range(2):
        keep_copy(which).wait()
    for which in range(2):
        for step in range(1, N_TP):
            tp_copy(which, step).wait_send()

        def sent(step, _):
            page_copy(which, step).wait_send()
            return 0

        lax.fori_loop(1, N_SEQ, sent, 0)
    for other_y in range(4):

        @pl.when(q_dest(other_y) != me)
        def _():
            q_remote(other_y).wait_send()

    for side in range(2):

        @pl.when(home + side != me)
        def _():
            f_remote(side).wait_send()


def merge_kernel(key_in, value_in, parts, stats, key_out, value_out, attended):
    key_out[...] = key_in[...]
    value_out[...] = value_in[...]
    logs = [stats[slot] for slot in range(4)]
    top = jnp.maximum(jnp.maximum(logs[0], logs[1]), jnp.maximum(logs[2], logs[3]))
    shares = [jnp.exp2(log - top) for log in logs]
    whole = 1.0 / (shares[0] + shares[1] + shares[2] + shares[3])
    shares = [share * whole for share in shares]
    lane = lax.broadcasted_iota(jnp.int32, (BLOCK, HD), 1)
    for index in range(HEADS // 2):
        mine = lane == pl.program_id(0) * (HEADS // 2) + index
        result = sum(
            parts[slot, index].astype(jnp.float32)
            * jnp.sum(jnp.where(mine, shares[slot], 0.0), axis=1, keepdims=True)
            for slot in range(4)
        )
        attended[:, index * HD : (index + 1) * HD] = result.astype(jnp.bfloat16)


def on_device(
    pool_keys,
    pool_values,
    passage_ids,
    page_slot,
    offsets,
    recompute_blocks,
    hidden_rows,
    w_key,
    w_value,
    queries,
):
    rates = jnp.asarray(frequencies())
    vmem = pl.BlockSpec(memory_space=pltpu.VMEM)
    smem = pl.BlockSpec(memory_space=pltpu.SMEM)
    hbm = pl.BlockSpec(memory_space=pltpu.HBM)
    bf16 = jnp.bfloat16
    dma = pltpu.SemaphoreType.DMA
    cache = jax.ShapeDtypeStruct((TOK_DEV, WIDTH), bf16)
    made = pl.pallas_call(
        blend_kernel,
        out_shape=[
            cache,
            cache,
            jax.ShapeDtypeStruct((4, HEADS, BLOCK, HD), bf16),
            jax.ShapeDtypeStruct((4, BLOCK, HD), jnp.float32),
        ],
        in_specs=[smem, hbm, smem, smem, vmem, hbm, hbm, hbm, hbm, hbm, hbm],
        out_specs=[hbm, hbm, hbm, hbm],
        scratch_shapes=[
            pltpu.VMEM((BLOCK, HEADS * HD), bf16),
            pltpu.VMEM((32, HD), jnp.int32),
            pltpu.VMEM((4, HEADS, BLOCK, HD), bf16),
            pltpu.VMEM((128, PAGE, WIDTH), bf16),
            pltpu.VMEM((128, PAGE, WIDTH), bf16),
            pltpu.VMEM((2, N_SEQ, CAP, PAGE, WIDTH), bf16),
            pltpu.VMEM((N_SEQ, CAP, PAGE, WIDTH), bf16),
            pltpu.VMEM((N_SEQ, CAP, PAGE, WIDTH), bf16),
            pltpu.VMEM((HEADS, BLOCK, HD), bf16),
            pltpu.VMEM((2, BLOCK, WIDTH), bf16),
            pltpu.VMEM((RB, 2, BLOCK, WIDTH), bf16),
            pltpu.VMEM((BLOCK, 8192), bf16),
            pltpu.VMEM((2, 8192, WIDTH), bf16),
            pltpu.VMEM((TOK_DEV, HD), jnp.float32),
            pltpu.VMEM((TOK_DEV, HD), jnp.float32),
            pltpu.VMEM((PASSAGES, HD), jnp.int32),
            pltpu.VMEM((PASSAGES, HD), jnp.int32),
            pltpu.VMEM((8, HD), jnp.int32),
            pltpu.SMEM((PASSAGES, HD), jnp.int32),
            pltpu.SMEM((8, HD), jnp.int32),
            pltpu.VMEM((4, 2, TOK_DEV, WIDTH), bf16),
            pltpu.VMEM((4, 2, TOK_DEV, WIDTH), bf16),
            pltpu.VMEM((4, HEADS, BLOCK, 2 * HD), jnp.float32),
            pltpu.VMEM((4, HEADS, BLOCK, HD), jnp.float32),
            pltpu.VMEM((4, HEADS, BLOCK, HD), bf16),
            pltpu.VMEM((4, BLOCK, HD), jnp.float32),
            dma((2,)),
            dma((7,)),
            dma((2, N_TP)),
            dma((2, N_TP)),
            dma((2, N_SEQ)),
            dma((2, N_SEQ)),
            dma((4,)),
            dma((4,)),
            dma((2,)),
            dma((2,)),
            dma((2,)),
            dma((2, 4)),
            dma((2, 4)),
            dma((2, 4)),
            dma((2, 4)),
            dma((2, 4)),
            dma((2, 4)),
        ],
        compiler_params=pltpu.CompilerParams(
            collective_id=0, has_side_effects=True, vmem_limit_bytes=60 * 2**20
        ),
        name="blend_and_attend",
    )(
        passage_ids, page_slot, offsets, recompute_blocks.T, rates,
        pool_keys, pool_values, hidden_rows, w_key, w_value, queries,
    )
    slab = pl.BlockSpec((TOK_DEV // 2, WIDTH), lambda i: (i, 0))
    return tuple(
        pl.pallas_call(
            merge_kernel,
            out_shape=[cache, cache, jax.ShapeDtypeStruct((BLOCK, HEADS * HD), bf16)],
            grid=(2,),
            in_specs=[
                slab,
                slab,
                pl.BlockSpec((4, HEADS // 2, BLOCK, HD), lambda i: (0, i, 0, 0)),
                pl.BlockSpec((4, BLOCK, HD), lambda i: (0, 0, 0)),
            ],
            out_specs=[slab, slab, pl.BlockSpec((BLOCK, HEADS * HD // 2), lambda i: (0, i))],
            name="merge",
        )(*made)
    )


def solution(mesh):
    placed = (
        P(("seq", "tp"), None, None),
        P(("seq", "tp"), None, None),
        P(),
        P(),
        P(),
        P(),
        P("seq", None),
        P(None, "tp"),
        P(None, "tp"),
        P("seq", "tp"),
    )
    return jax.shard_map(
        on_device,
        mesh=mesh,
        in_specs=placed,
        out_specs=(P("seq", "tp"), P("seq", "tp"), P("seq", "tp")),
        check_vma=False,
    )
```
